32 devices in a mesh: gx: 8 (over y, x, core), gy: 4 (over z).
Axes of the slice: x: 2, y: 2, z: 4, core: 2. Of those that a mesh axis runs over, the one named last changes fastest.
Arguments:
- incident: float32 [18, 10, 256, 512], P(None, None, 'gx', 'gy'), may hold values from -6 to 6
- cotangent: float32 [18, 10, 256, 512], P(None, None, 'gx', 'gy'), may hold values from -6 to 6
- scatter_table: float32 [4, 18, 18], replicated, may hold values from -1.5 to 1.5
- deriv_table: float32 [4, 18, 18], replicated, may hold values from -1.5 to 1.5
- material_code: int32 [10, 256, 64], P(None, 'gx', 'gy'), may hold values from 0 to 3
- boundary_code: int32 [2, 256, 64], P(None, 'gx', 'gy'), may hold values from 0 to 2
- param_ids: int32 [256, 512], P('gx', 'gy'), may hold values from 0 to 131071, as said below
Outputs:
- adjoint_field: float32 [18, 10, 256, 512], P(None, None, 'gx', 'gy')
- sensitivity: float32 [131072], P(('gx', 'gy'))
The draws below stay inside these ranges and needn't reach their ends.
Inputs may be any that keep to these rules, and one draw needn't show every extreme that they name: `param_ids`: parameter i belongs to device i // 4096 of gx+gy, gy fastest. The columns of one device name parameters of any one owner at most 256 times, and on every device some owner is named exactly 256 times.
All inputs are finite; a program needn't handle non-finite values.
Results may differ from the reference program's by a relative error of at most 0.0001.
Values sent between devices are 32-bit elements; how exact they have to be, the bound alone decides.
No kernel may reach another device: no remote copies, remote signals or barrier semaphores. Data moves between devices by JAX's collectives and lax.ppermute only.
A program may use at most 128 MiB of HBM per device.

```python
import jax
import jax.numpy as jnp
from jax import lax

NPORT = 18
NMAT = 4
BW = 8
CZ = 10
ITERS = 4
CX = 32
CY = 128
NX = 256
NY = 512
P_DEV = 4096
PARAMS = 131072
CAP = 256
N_GX = 8
N_GY = 4
DEVICES = 32


def device_owners(key):
    keys = jax.random.split(key, 4)
    full_owner = jax.random.randint(keys[0], (), 0, DEVICES).astype(jnp.int32)
    slots = jax.random.permutation(keys[1], (DEVICES - 1) * CAP)[:CX * CY - CAP].astype(jnp.int32)
    others = slots // CAP
    others = others + (others >= full_owner).astype(jnp.int32)
    owners = jnp.concatenate([jnp.zeros((CAP,), jnp.int32) + full_owner, others])
    owners = owners[jax.random.permutation(keys[2], CX * CY)]
    local = jax.random.randint(keys[3], (CX * CY,), 0, P_DEV).astype(jnp.int32)
    return (owners * P_DEV + local).reshape(CX, CY)


def draw_param_ids(key, part):
    keys = jax.random.split(jax.random.fold_in(key, 7), DEVICES)
    blocks = jax.vmap(device_owners)(keys)
    blocks = blocks.reshape(N_GX, N_GY, CX, CY).transpose(0, 2, 1, 3)
    return blocks.reshape(NX, NY).astype(jnp.int32)


def with_ends(values, stream_key, least, largest):
    dims = values.shape
    index_at = [jax.random.randint(jax.random.fold_in(stream_key, axis), (), 0, dims[axis]) for axis in range(len(dims))]
    values = values.at[tuple(index_at)].set(least)
    longest = dims.index(max(dims))
    index_at[longest] = (index_at[longest] + 1) % dims[longest]
    return values.at[tuple(index_at)].set(largest)


def steps_of(rng, shape, cuts, low, high):
    def one(position, blocks):
        steps = jax.random.uniform(jax.random.fold_in(jax.random.fold_in(rng, 6), position), (blocks,), jnp.float32, low / len(cuts), high / len(cuts))
        return jnp.repeat(jnp.exp(steps), shape[position] // blocks).reshape((-1,) + (1,) * (len(shape) - position - 1))

    level = one(*cuts[0])
    for cut in cuts[1:]:
        level = level * one(*cut)
    return level


def normal_values(stream_key, shape, scale, limit, pieces=(), kind=jnp.bfloat16):
    array = jax.random.normal(stream_key, shape, jnp.float32) * scale
    if len(pieces) > 0:
        array = steps_of(stream_key, shape, pieces, -0.22, 0.18) * array
    return jnp.clip(array, min=-limit, max=limit).astype(kind)


def setup_inputs(seed: int = 0) -> dict:
    arg_keys = jax.random.split(jax.random.key(seed), 8)
    return {
        "incident": normal_values(arg_keys[0], (NPORT, CZ, NX, NY), 1.0, 6.0, ((2, 8), (3, 4)), jnp.float32),
        "cotangent": normal_values(arg_keys[1], (NPORT, CZ, NX, NY), 1.0, 6.0, ((2, 8), (3, 4)), jnp.float32),
        "scatter_table": normal_values(arg_keys[2], (NMAT, NPORT, NPORT), NPORT ** -0.5, 1.5, (), jnp.float32),
        "deriv_table": normal_values(arg_keys[3], (NMAT, NPORT, NPORT), NPORT ** -0.5, 1.5, (), jnp.float32),
        "material_code": with_ends(jax.random.randint(arg_keys[4], (CZ, NX, NY // BW), 0, NMAT), jax.random.fold_in(arg_keys[4], 1), 0, NMAT - 1).astype(jnp.int32),
        "boundary_code": with_ends(jax.random.randint(arg_keys[5], (2, NX, NY // BW), 0, 3), jax.random.fold_in(arg_keys[5], 1), 0, 2).astype(jnp.int32),
        "param_ids": draw_param_ids(jax.random.fold_in(arg_keys[7], 71), 0),
    }


sens_scale = 1.0 / 32.0


def end_coefficient(codes):
    return jnp.where(codes == 0, -1.0, jnp.where(codes == 1, 1.0, 0.0)).astype(jnp.float32)


def connect(reflected, lower_coef, upper_coef):
    east = reflected[0:2]
    west = reflected[2:4]
    north = reflected[4:6]
    south = reflected[6:8]
    upper = reflected[8:10]
    lower = reflected[10:12]
    new_west = jnp.roll(east, 1, axis=2)
    new_east = jnp.roll(west, -1, axis=2)
    new_south = jnp.concatenate([-south[..., :1], north[..., :-1]], axis=3)
    new_north = jnp.concatenate([south[..., 1:], -north[..., -1:]], axis=3)
    new_lower = jnp.concatenate([lower_coef * lower[:, :1], upper[:, :-1]], axis=1)
    new_upper = jnp.concatenate([lower[:, 1:], upper_coef * upper[:, -1:]], axis=1)
    return jnp.concatenate([new_east, new_west, new_north, new_south, new_upper, new_lower, reflected[12:]], axis=0)


def apply_table(table, cells, field, transpose):
    form = "qp,qzxy->pzxy" if transpose else "pq,qzxy->pzxy"
    total = jnp.zeros_like(field)
    for index in range(table.shape[0]):
        product = jnp.einsum(form, table[index], field, precision=lax.Precision.HIGHEST)
        total = total + jnp.where(cells[None] == index, product, 0.0)
    return total


def reference(incident, cotangent, scatter_table, deriv_table, material_code, boundary_code, param_ids):
    cells = jnp.repeat(material_code, BW, axis=2)
    lower_coef = end_coefficient(jnp.repeat(boundary_code[0], BW, axis=1))[None, None]
    upper_coef = end_coefficient(jnp.repeat(boundary_code[1], BW, axis=1))[None, None]
    field = incident
    saved = []
    for step in range(ITERS):
        saved.append(field)
        field = connect(apply_table(scatter_table, cells, field, False), lower_coef, upper_coef)
    adjoint = cotangent
    column = jnp.zeros((NX, NY), jnp.float32)
    for step in reversed(range(ITERS)):
        reflected = connect(adjoint, lower_coef, upper_coef)
        change = apply_table(deriv_table, cells, saved[step], False)
        column = column + jnp.sum(reflected * change, axis=(0, 1))
        adjoint = apply_table(scatter_table, cells, reflected, True)
    sensitivity = jax.ops.segment_sum(column.reshape(-1), param_ids.reshape(-1), num_segments=PARAMS) * sens_scale
    return adjoint, sensitivity
```

```python
import functools

import jax
import jax.numpy as jnp
from jax import lax
from jax.experimental import pallas as pl
from jax.experimental.pallas import tpu as pltpu
from jax.sharding import PartitionSpec as P

BW = 8
ITERS = 4
HALO = 4
SUB = 8
LANES = 128
GROUP = LANES // (2 * HALO)
MSG = 40
ROWS = 24
KDIM = 144
F32 = jnp.float32
BF16 = jnp.bfloat16
sens_scale = 1.0 / 32.0
MIB = 2**20
VMEM = pl.BlockSpec(memory_space=pltpu.VMEM)
SMEM = pl.BlockSpec(memory_space=pltpu.SMEM)
ANY = pl.BlockSpec(memory_space=pl.ANY)


def iota(shape, dim):
    return lax.broadcasted_iota(jnp.int32, shape, dim)


def roll(value, amount, axis):
    return pltpu.roll(value, amount, axis)


def shifted(block):
    row = iota((SUB, LANES), 0)
    up = roll(block, LANES - 1, 1)
    down = roll(block, 1, 1)
    return jnp.where(row < 4, block, jnp.where(row < 6, up, down))


def swap_pairs(block):
    row = iota((SUB, LANES), 0)
    return jnp.where(row % 4 < 2, roll(block, SUB - 2, 0), roll(block, 2, 0))


def swap_first(block):
    row = iota((SUB, LANES), 0)
    return jnp.where(row < 4, swap_pairs(block), block)


def pack_kernel(inc, cot, mat, low, high, pk, es, xl, xr):
    z = pl.program_id(0)
    cz = pl.num_programs(0)
    nx = inc.shape[2]
    lane = iota((SUB, LANES), 1)
    row = iota((SUB, LANES), 0)
    spread = (iota((mat.shape[2], LANES), 1) // BW == iota((mat.shape[2], LANES), 0)).astype(BF16)

    def expand(codes):
        return jnp.dot(codes.astype(F32).astype(BF16), spread, preferred_element_type=F32)

    def coefficient(codes):
        return jnp.where(codes == 0, -1.0, jnp.where(codes == 1, 1.0, 0.0))

    code = expand(mat[0])
    lower = expand(coefficient(low[0]))
    upper = expand(coefficient(high[0]))
    ends = jnp.where(z == 0, lower, jnp.where(z == cz - 1, upper, 0.0))
    flat_inc = inc.reshape(inc.shape[0] * nx, LANES)
    flat_cot = cot.reshape(cot.shape[0] * nx, LANES)
    for half in range(nx // GROUP):
        edge = [jnp.zeros((SUB, LANES), F32) for _ in range(5)]
        for g in range(GROUP):
            x = half * GROUP + g
            f0 = flat_inc[pl.ds(x, 8, stride=nx), :]
            f1 = flat_inc[pl.ds(8 * nx + x, 8, stride=nx), :]
            a0 = swap_pairs(flat_cot[pl.ds(x, 8, stride=nx), :])
            a1 = swap_first(flat_cot[pl.ds(8 * nx + x, 8, stride=nx), :])
            last = [
                flat_inc[pl.ds(16 * nx + x, 1), :],
                flat_inc[pl.ds(17 * nx + x, 1), :],
                flat_cot[pl.ds(16 * nx + x, 1), :],
                flat_cot[pl.ds(17 * nx + x, 1), :],
                code[x : x + 1],
                ends[x : x + 1],
            ]
            tail = jnp.zeros((SUB, LANES), F32)
            for i, value in enumerate(last):
                tail = jnp.where(row == i, jnp.broadcast_to(value, (SUB, LANES)), tail)
            mine = lane // (2 * HALO) == g
            for i, value in enumerate((f0, f1, a0, a1, tail)):
                edge[i] = jnp.where(mine, roll(value, 2 * HALO * g + HALO, 1), edge[i])
            for i, value in enumerate((f0, f1, shifted(a0), a1, tail)):
                pk[0, x, pl.ds(8 * i, 8), :] = value
                if x < HALO:
                    xl[0, x, pl.ds(8 * i, 8), :] = value
                if x >= nx - HALO:
                    xr[0, x - nx + HALO, pl.ds(8 * i, 8), :] = value
        for i in range(5):
            es[0, half, pl.ds(8 * i, 8), :] = edge[i]


def pack(incident, cotangent, material, lower, upper):
    ports, cz, nx, ny = incident.shape
    halves = nx // GROUP
    field = pl.BlockSpec((ports, 1, nx, ny), lambda z: (0, z, 0, 0))
    codes = pl.BlockSpec((1, nx, material.shape[2]), lambda z: (z, 0, 0))
    ends = pl.BlockSpec((1, nx, material.shape[2]), lambda z: (0, 0, 0))

    def out(rows):
        return pl.BlockSpec((1, rows, MSG, LANES), lambda z: (z, 0, 0, 0))

    def shape(rows):
        return jax.ShapeDtypeStruct((cz, rows, MSG, LANES), F32)

    sizes = (nx, halves, HALO, HALO)
    return pl.pallas_call(
        pack_kernel,
        grid=(cz,),
        in_specs=[field, field, codes, ends, ends],
        out_specs=[out(n) for n in sizes],
        out_shape=[shape(n) for n in sizes],
        compiler_params=pltpu.CompilerParams(vmem_limit_bytes=24 * MIB),
        name="pack",
    )(incident, cotangent, material, lower, upper)


def build_tables(scatter, deriv, tables):
    nmat, ports, _ = scatter.shape
    r = iota((ROWS, ports), 0)
    c = iota((ROWS, ports), 1)
    tail = (r >= 16) & (c == 16 + r % 2)
    natural = (((r < 16) & (r == c)) | tail).astype(F32).astype(BF16)
    swapped_port = jnp.where(r < 12, r + jnp.where(r % 4 < 2, 2, -2), r)
    permuted = (((r < 16) & (swapped_port == c)) | tail).astype(F32).astype(BF16)
    plain = (r == c).astype(F32).astype(BF16)
    q = iota((ports, KDIM), 0)
    k = iota((ports, KDIM), 1)

    def place(m):
        main = (k < 128) & ((k // 16) % 4 == m) & (q == k % 16)
        end = (k >= 128) & ((k % 8) // 2 == m) & (q == 16 + k % 2)
        return (main | end).astype(F32).astype(BF16)

    places = [place(m) for m in range(nmat)]

    def split(value):
        high = value.astype(BF16)
        return high, (value - high.astype(F32)).astype(BF16)

    def form(table, rows, transpose):
        parts = []
        for part in range(2):
            total = jnp.zeros((ROWS, KDIM), F32)
            for m in range(nmat):
                piece = split(table[m])[part]
                axes = (((1,), (1 if transpose else 0,)), ((), ()))
                picked = lax.dot_general(rows, piece, axes, preferred_element_type=F32).astype(BF16)
                total = total + jnp.dot(picked, places[m], preferred_element_type=F32)
            parts.append(total.astype(BF16))
        return parts

    forms = (
        form(scatter, permuted, False)
        + form(deriv, plain, False)
        + form(scatter, permuted, True)
        + form(scatter, natural, True)
    )
    for i, value in enumerate(forms):
        tables[pl.ds(ROWS * i, ROWS), :] = value.astype(F32)


def main_kernel(
    flags, scatter, deriv, pk, fl, fr, hl, hr,
    adjoint, column,
    rf, ra, rtail, masks, saved_d, saved_r, xf, xa, tf, ta, acc, tables, ebuf, sems,
):
    cz, nx = pk.shape[0], pk.shape[1]
    ne = nx + 2 * HALO
    nb = rf.shape[2] - ne
    row = iota((SUB, LANES), 0)
    lane = iota((SUB, LANES), 1)
    is_first = flags[0] == 1
    is_last = flags[1] == 1

    copies = []
    for i, (source, first, count) in enumerate(((pk, HALO, nx), (hl, 0, HALO), (hr, HALO + nx, HALO))):
        src = source.at[:, pl.ds(0, count)]
        for j, (target, at, size) in enumerate(
            ((rf.at[0, :, pl.ds(first, count), pl.ds(0, 16)], 0, 16),
             (ra.at[0, :, pl.ds(first, count), pl.ds(0, 16)], 16, 16),
             (rtail.at[:, pl.ds(first, count)], 32, 8))
        ):
            copies.append(pltpu.make_async_copy(src.at[:, :, pl.ds(at, size)], target, sems.at[3 * i + j]))
    for copy in copies:
        copy.start()
    build_tables(scatter, deriv, tables)

    def halo_blocks(z, _):
        for i in range(5):
            part = pl.ds(8 * i, 8)
            blocks = [
                roll(jnp.where(lane % 8 < HALO, fl[z, h, part, :], fr[z, h, part, :]), 8 * HALO, 1)
                for h in range(nb - 1)
            ]
            for b in range(nb):
                before = hl[z, HALO, part, :] if b == 0 else blocks[b - 1]
                after = hr[z, HALO, part, :] if b == nb - 1 else blocks[b]
                value = jnp.where(lane < 8 * HALO, before, after)
                if i == 0 or i == 1:
                    rf[0, z, ne + b, part, :] = value
                elif i == 2:
                    ra[0, z, ne + b, pl.ds(0, 8), :] = shifted(value)
                elif i == 3:
                    ra[0, z, ne + b, pl.ds(8, 8), :] = value
                else:
                    rtail[z, ne + b] = value
        return 0

    lax.fori_loop(0, cz, halo_blocks, 0)
    for copy in copies:
        copy.wait()

    def repeated(value):
        value = jnp.where(row < 2, value, 0.0)
        value = value + roll(value, 2, 0)
        return value + roll(value, 4, 0)

    wide_row = iota((16, LANES), 0)

    def start_rows(r, _):
        for z in range(cz):
            t = rtail[z, r]
            rf[0, z, r, pl.ds(16, 8), :] = repeated(t)
            ra[0, z, r, pl.ds(16, 8), :] = repeated(roll(t, 6, 0))
            code = jnp.broadcast_to(rtail[z, r, pl.ds(4, 1), :], (16, LANES))
            for m in range(4):
                masks[z, r, pl.ds(16 * m, 16), :] = jnp.where(code == m, 1.0, 0.0).astype(BF16)
            own = ((wide_row % 8) // 2).astype(F32)
            masks[z, r, pl.ds(64, 16), :] = jnp.where(code == own, 1.0, 0.0).astype(BF16)
        return 0

    lax.fori_loop(0, ne + nb, start_rows, 0)

    def operand(values, z, r):
        v0, v1, v2 = values
        main = jnp.concatenate([v0, v1], axis=0)
        high = main.astype(BF16)
        low = (main - high.astype(F32)).astype(BF16)
        high2 = v2.astype(BF16).astype(F32)
        end = jnp.concatenate([high2, v2 - high2], axis=0).astype(BF16)
        mask = [masks[z, r, pl.ds(16 * m, 16), :] for m in range(5)]
        pieces = [high * mask[m] for m in range(4)] + [low * mask[m] for m in range(4)]
        return jnp.concatenate(pieces + [end * mask[4]], axis=0)

    def apply(table, values, r):
        outs = []
        for z in range(0, cz, 2):
            rhs = jnp.concatenate([operand(values[z], z, r), operand(values[z + 1], z + 1, r)], axis=1)
            y = jnp.dot(table, rhs, preferred_element_type=F32)
            for h in range(2):
                part = y[:, h * LANES : (h + 1) * LANES]
                outs.append([
                    [part[at + 8 * i : at + 8 * i + 8] + part[at + ROWS + 8 * i : at + ROWS + 8 * i + 8] for i in range(3)]
                    for at in range(0, table.shape[0], 2 * ROWS)
                ])
        return outs

    def read(ref, slot, r):
        return [[ref[slot, z, r, pl.ds(8 * i, 8), :] for i in range(3)] for z in range(cz)]

    def along_z(values, r):
        low = jnp.broadcast_to(rtail[0, r, pl.ds(5, 1), :], (SUB, LANES))
        high = jnp.broadcast_to(rtail[cz - 1, r, pl.ds(5, 1), :], (SUB, LANES))
        outs = []
        for z in range(cz):
            own = values[z][1]
            above = values[z + 1][1] if z + 1 < cz else high * roll(own, 6, 0)
            below = values[z - 1][1] if z > 0 else low * roll(own, 2, 0)
            outs.append(jnp.where(row < 2, above, jnp.where(row < 4, below, own)))
        return outs

    at_ends = ((row // 2 == 2) & (lane == LANES - 1)) | ((row // 2 == 3) & (lane == 0))
    at_edges = ((row // 2 == 2) & (lane % 8 == HALO - 1)) | ((row // 2 == 3) & (lane % 8 == HALO))

    def connect_row(ref, slot, tm, e):
        values = read(ref, slot, e)
        planes = along_z(values, e)
        amount = LANES - (8 * (e % GROUP) + HALO)
        outs = []
        for z in range(cz):
            after = ref[slot, z, e + 1, pl.ds(0, 8), :]
            before = ref[slot, z, e - 1, pl.ds(0, 8), :]
            outer = roll(tm[z, e // GROUP], amount, 1)
            own = jnp.where(at_ends, outer, values[z][0])
            outs.append([jnp.where(row < 2, after, jnp.where(row < 4, before, own)), planes[z], values[z][2]])
        return outs

    def connect_edge(ref, slot, x, tm, b):
        r = ne + b
        values = read(ref, slot, r)
        planes = along_z(values, r)
        outs = []
        for z in range(cz):
            own = values[z][0]
            nxt = ref[slot, z, ne + (b + 1) % nb, pl.ds(0, 8), :]
            prv = ref[slot, z, ne + (b + nb - 1) % nb, pl.ds(0, 8), :]
            after = roll(jnp.where(lane >= 8, own, nxt), LANES - 8, 1)
            before = roll(jnp.where(lane < LANES - 8, own, prv), 8, 1)
            inner = x[z, b]
            top = roll(roll(inner, LANES - 1, 1), 6, 0)
            bottom = roll(roll(inner, 1, 1), 2, 0)
            tm[z, b] = jnp.where(
                is_last & (row < 6), -top, jnp.where(is_first & (row >= 6), -bottom, own)
            )
            own = jnp.where(at_edges, inner, own)
            outs.append([jnp.where(row < 2, after, jnp.where(row < 4, before, own)), planes[z], values[z][2]])
        return outs

    def collect(x, e, blocks):
        g = e % GROUP
        for z in range(cz):
            moved = roll(blocks[z], 8 * g + HALO, 1)
            x[z, e // GROUP] = jnp.where(lane // 8 == g, moved, x[z, e // GROUP])

    def write(ref, slot, r, z, part):
        first = shifted(part[0])
        ref[slot, z, r, pl.ds(0, 8), :] = first
        ref[slot, z, r, pl.ds(8, 8), :] = part[1]
        ref[slot, z, r, pl.ds(16, 8), :] = part[2]
        return first

    for x in (xf, xa):
        x[...] = jnp.zeros_like(x)

    def gather_first(e, _):
        collect(xa, e, [ra[0, z, e, pl.ds(0, 8), :] for z in range(cz)])
        return 0

    lax.fori_loop(0, ne, gather_first, 0)
    flat = adjoint.reshape(adjoint.shape[0] * cz * nx, LANES)

    def product(e, left, right):
        total = acc[e]
        for z in range(cz):
            for i in range(3):
                total = total + left[z][i] * right(z, i)
        acc[e] = total

    for step in range(ITERS):
        slot, other = step % 2, (step + 1) % 2
        last = step == ITERS - 1
        s_table = tables[pl.ds(0, 2 * ROWS), :].astype(BF16)
        sd_table = tables[pl.ds(0, 4 * ROWS), :].astype(BF16)
        d_table = tables[pl.ds(2 * ROWS, 2 * ROWS), :].astype(BF16)
        a_table = tables[pl.ds((6 if last else 4) * ROWS, 2 * ROWS), :].astype(BF16)

        def edges(b, _, step=step, slot=slot, other=other, last=last, s_table=s_table, a_table=a_table):
            av = connect_edge(ra, slot, xa, ta, b)
            fv = connect_edge(rf, slot, xf, tf, b) if step > 0 else read(rf, slot, ne + b)
            if not last:
                for z, parts in enumerate(apply(a_table, av, ne + b)):
                    write(ra, other, ne + b, z, parts[0])
                for z, parts in enumerate(apply(s_table, fv, ne + b)):
                    write(rf, other, ne + b, z, parts[0])
            return 0

        lax.fori_loop(0, nb, edges, 0)

        def rows(e, _, step=step, slot=slot, other=other, last=last, sd_table=sd_table, d_table=d_table, a_table=a_table):
            av = connect_row(ra, slot, ta, e)
            fv = connect_row(rf, slot, tf, e) if step > 0 else read(rf, slot, e)
            a_out = apply(a_table, av, e)
            if last:
                for z in range(cz):
                    part = a_out[z][0]
                    at = z * nx + e - HALO
                    flat[pl.ds(at, 8, stride=cz * nx), :] = part[0]
                    flat[pl.ds(8 * cz * nx + at, 8, stride=cz * nx), :] = part[1]
                    flat[pl.ds(16 * cz * nx + at, 1), :] = part[2][0:1]
                    flat[pl.ds(17 * cz * nx + at, 1), :] = part[2][1:2]
                change = [parts[0] for parts in apply(d_table, fv, e)]
            else:
                collect(xa, e, [write(ra, other, e, z, a_out[z][0]) for z in range(cz)])
                f_out = apply(sd_table, fv, e)
                collect(xf, e, [write(rf, other, e, z, f_out[z][0]) for z in range(cz)])
                change = [parts[1] for parts in f_out]
            if step < 2:
                for z in range(cz):
                    for i in range(3):
                        saved_r[step, z, e, pl.ds(8 * i, 8), :] = av[z][i]
                        saved_d[step, z, e, pl.ds(8 * i, 8), :] = change[z][i]
            else:
                k = ITERS - 1 - step
                product(e, av, lambda z, i: saved_d[k, z, e, pl.ds(8 * i, 8), :])
                product(e, change, lambda z, i: saved_r[k, z, e, pl.ds(8 * i, 8), :])
            return 0

        if step == 0:
            acc[...] = jnp.zeros_like(acc)
        lax.fori_loop(1 + step, ne - 1 - step, rows, 0)

    for x in range(nx):
        column[pl.ds(x, 1), :] = jnp.sum(acc[HALO + x], axis=0, keepdims=True) * sens_scale


def main_call(flags, scatter, deriv, pk, fl, fr, hl, hr):
    cz, nx = pk.shape[0], pk.shape[1]
    ports = scatter.shape[1]
    ne = nx + 2 * HALO
    nb = ne // GROUP + 1
    total = ne + nb
    return pl.pallas_call(
        main_kernel,
        in_specs=[SMEM, VMEM, VMEM, ANY, VMEM, VMEM, VMEM, VMEM],
        out_specs=[VMEM, VMEM],
        out_shape=[
            jax.ShapeDtypeStruct((ports, cz, nx, LANES), F32),
            jax.ShapeDtypeStruct((nx, LANES), F32),
        ],
        scratch_shapes=[
            pltpu.VMEM((2, cz, total, ROWS, LANES), F32),
            pltpu.VMEM((2, cz, total, ROWS, LANES), F32),
            pltpu.VMEM((cz, total, SUB, LANES), F32),
            pltpu.VMEM((cz, total, 80, LANES), BF16),
            pltpu.VMEM((2, cz, ne, ROWS, LANES), F32),
            pltpu.VMEM((2, cz, ne, ROWS, LANES), F32),
            pltpu.VMEM((cz, nb, SUB, LANES), F32),
            pltpu.VMEM((cz, nb, SUB, LANES), F32),
            pltpu.VMEM((cz, nb, SUB, LANES), F32),
            pltpu.VMEM((cz, nb, SUB, LANES), F32),
            pltpu.VMEM((ne, SUB, LANES), F32),
            pltpu.VMEM((8 * ROWS, KDIM), F32),
            pltpu.VMEM((SUB, LANES), F32),
            pltpu.SemaphoreType.DMA((9,)),
        ],
        compiler_params=pltpu.CompilerParams(vmem_limit_bytes=63 * MIB),
        name="adjoint_steps",
    )(flags, scatter, deriv, pk, fl, fr, hl, hr)


def route_kernel(ids, owner_hot, rank_hot, id_slots):
    nx = ids.shape[0]
    ndev, cap = id_slots.shape
    owned = nx * LANES
    who = iota((ndev, LANES), 0)
    place = iota((cap, LANES), 0)
    before = (iota((LANES, LANES), 0) < iota((LANES, LANES), 1)).astype(BF16)
    offset = jnp.zeros((ndev, 1), F32)
    id_slots[...] = jnp.zeros_like(id_slots)
    for x in range(nx):
        wanted = ids[pl.ds(x, 1), :]
        hot = (wanted // owned == who).astype(F32)
        counts = jnp.dot(hot.astype(BF16), before, preferred_element_type=F32) + offset
        rank = jnp.sum(hot * counts, axis=0, keepdims=True).astype(jnp.int32)
        ranked = (rank == place).astype(F32).astype(BF16)
        offset = offset + jnp.sum(hot, axis=1, keepdims=True)
        local = wanted % owned
        owner_hot[:, pl.ds(x * LANES, LANES)] = hot.astype(BF16)
        rank_hot[:, pl.ds(x * LANES, LANES)] = ranked
        high = (hot * (local // 64).astype(F32)).astype(BF16)
        low = (hot * (local % 64).astype(F32)).astype(BF16)
        both = lax.dot_general(
            jnp.concatenate([high, low], axis=0), ranked, (((1,), (1,)), ((), ())), preferred_element_type=F32
        )
        id_slots[...] += 64.0 * both[:ndev] + both[ndev:]


def route(ids, ndev, cap):
    n = ids.shape[0] * ids.shape[1]
    return pl.pallas_call(
        route_kernel,
        in_specs=[VMEM],
        out_specs=[VMEM] * 3,
        out_shape=[
            jax.ShapeDtypeStruct((ndev, n), BF16),
            jax.ShapeDtypeStruct((cap, n), BF16),
            jax.ShapeDtypeStruct((ndev, cap), F32),
        ],
        compiler_params=pltpu.CompilerParams(vmem_limit_bytes=24 * MIB),
        name="route",
    )(ids)


def send_kernel(column, owner_hot, rank_hot, id_slots, message):
    nx = column.shape[0]
    ndev, cap = id_slots.shape
    total = jnp.zeros((2 * ndev, cap), F32)
    for x in range(nx):
        value = jnp.broadcast_to(column[pl.ds(x, 1), :], (ndev, LANES))
        high = value.astype(BF16)
        low = (value - high.astype(F32)).astype(BF16)
        part = pl.ds(x * LANES, LANES)
        hot = owner_hot[:, part]
        total = total + lax.dot_general(
            jnp.concatenate([high * hot, low * hot], axis=0), rank_hot[:, part],
            (((1,), (1,)), ((), ())), preferred_element_type=F32,
        )
    message[:, pl.ds(0, cap)] = total[:ndev] + total[ndev:]
    message[:, pl.ds(cap, cap)] = id_slots[...]


def send(column, owner_hot, rank_hot, id_slots):
    ndev, cap = id_slots.shape
    return pl.pallas_call(
        send_kernel,
        in_specs=[VMEM] * 4,
        out_specs=VMEM,
        out_shape=jax.ShapeDtypeStruct((ndev, 2 * cap), F32),
        compiler_params=pltpu.CompilerParams(vmem_limit_bytes=24 * MIB),
        name="send",
    )(column, owner_hot, rank_hot, id_slots)


def gather_kernel(message, out):
    ndev, cap = message.shape[0], message.shape[1] // 2
    nrow = out.shape[0]
    rows = iota((nrow, cap), 0)
    lanes = iota((LANES, cap), 0)
    total = jnp.zeros((2 * nrow, LANES), F32)
    for s in range(ndev):
        value = jnp.broadcast_to(message[pl.ds(s, 1), pl.ds(0, cap)], (nrow, cap))
        local = message[pl.ds(s, 1), pl.ds(cap, cap)].astype(jnp.int32)
        high = value.astype(BF16).astype(F32)
        mine = local // LANES == rows
        left = jnp.concatenate([jnp.where(mine, high, 0.0), jnp.where(mine, value - high, 0.0)], axis=0)
        right = (local % LANES == lanes).astype(F32).astype(BF16)
        total = total + lax.dot_general(
            left.astype(BF16), right, (((1,), (1,)), ((), ())), preferred_element_type=F32
        )
    out[...] = total[:nrow] + total[nrow:]


def gather(message, owned):
    return pl.pallas_call(
        gather_kernel,
        in_specs=[VMEM],
        out_specs=VMEM,
        out_shape=jax.ShapeDtypeStruct((owned // LANES, LANES), F32),
        compiler_params=pltpu.CompilerParams(vmem_limit_bytes=24 * MIB),
        name="gather",
    )(message)


def moved(block, axis, distance, wrap):
    count = lax.axis_size(axis)
    pairs = [(i, (i + distance) % count) for i in range(count) if wrap or 0 <= i + distance < count]
    return lax.ppermute(block, axis, pairs)


def shards(incident, cotangent, scatter_table, deriv_table, material_code, boundary_code, param_ids):
    position = lax.axis_index("gy")
    extent = lax.axis_size("gy")
    ndev = lax.axis_size("gx") * extent
    owned = param_ids.shape[0] * param_ids.shape[1]
    cap = 2 * owned // ndev
    pk, es, xl, xr = pack(incident, cotangent, material_code, boundary_code[0:1], boundary_code[1:2])
    fl = moved(es, "gy", 1, False)
    fr = moved(es, "gy", -1, False)
    owner_hot, rank_hot, id_slots = route(param_ids, ndev, cap)
    near = (jnp.arange(LANES) % (2 * HALO) < HALO)[None, None, None]
    low = jnp.where(near, fl[:, :1], fr[:, :1])
    high = jnp.where(near, fl[:, -1:], fr[:, -1:])
    place = 8 * HALO
    low = jnp.roll(low, place, axis=3)
    high = jnp.roll(high, place, axis=3)
    hr = moved(jnp.concatenate([xl, low], axis=1), "gx", -1, True)
    hl = moved(jnp.concatenate([xr, high], axis=1), "gx", 1, True)
    flags = jnp.stack([position == 0, position == extent - 1]).astype(jnp.int32)
    adjoint, column = main_call(flags, scatter_table, deriv_table, pk, fl, fr, hl, hr)
    message = send(column, owner_hot, rank_hot, id_slots)
    received = lax.all_to_all(message, ("gx", "gy"), 0, 0, tiled=True)
    sensitivity = gather(received, owned).reshape(-1)
    return adjoint, sensitivity


def solution(mesh):
    in_specs = (
        P(None, None, "gx", "gy"),
        P(None, None, "gx", "gy"),
        P(),
        P(),
        P(None, "gx", "gy"),
        P(None, "gx", "gy"),
        P("gx", "gy"),
    )
    out_specs = (P(None, None, "gx", "gy"), P(("gx", "gy")))
    return jax.shard_map(shards, mesh=mesh, in_specs=in_specs, out_specs=out_specs, check_vma=False)
```

```python
import functools

import jax
import jax.numpy as jnp
from jax import lax
from jax.experimental import pallas as pl
from jax.experimental.pallas import tpu as pltpu
from jax.sharding import PartitionSpec as P

BW = 8
ITERS = 4
CHUNK = 8
HALO = 4
SUB = 8
LANES = 128
GROUP = LANES // (2 * HALO)
MSG = 40
ROWS = 24
KDIM = 144
F32 = jnp.float32
BF16 = jnp.bfloat16
sens_scale = 1.0 / 32.0
MIB = 2**20
VMEM = pl.BlockSpec(memory_space=pltpu.VMEM)
SMEM = pl.BlockSpec(memory_space=pltpu.SMEM)
ANY = pl.BlockSpec(memory_space=pl.ANY)


def iota(shape, dim):
    return lax.broadcasted_iota(jnp.int32, shape, dim)


def roll(value, amount, axis):
    return pltpu.roll(value, amount, axis)


def shifted(block):
    row = iota((SUB, LANES), 0)
    up = roll(block, LANES - 1, 1)
    down = roll(block, 1, 1)
    return jnp.where(row < 4, block, jnp.where(row < 6, up, down))


def swap_pairs(block):
    row = iota((SUB, LANES), 0)
    return jnp.where(row % 4 < 2, roll(block, SUB - 2, 0), roll(block, 2, 0))


def swap_first(block):
    row = iota((SUB, LANES), 0)
    return jnp.where(row < 4, swap_pairs(block), block)


def pack_kernel(inc, cot, mat, low, high, pk, es, xl, xr):
    z = pl.program_id(0)
    cz = pl.num_programs(0)
    nx = inc.shape[2]
    lane = iota((SUB, LANES), 1)
    row = iota((SUB, LANES), 0)
    spread = (iota((mat.shape[2], LANES), 1) // BW == iota((mat.shape[2], LANES), 0)).astype(BF16)

    def expand(codes):
        return jnp.dot(codes.astype(F32).astype(BF16), spread, preferred_element_type=F32)

    def coefficient(codes):
        return jnp.where(codes == 0, -1.0, jnp.where(codes == 1, 1.0, 0.0))

    code = expand(mat[0])
    lower = expand(coefficient(low[0]))
    upper = expand(coefficient(high[0]))
    ends = jnp.where(z == 0, lower, jnp.where(z == cz - 1, upper, 0.0))
    flat_inc = inc.reshape(inc.shape[0] * nx, LANES)
    flat_cot = cot.reshape(cot.shape[0] * nx, LANES)
    for half in range(nx // GROUP):
        edge = [jnp.zeros((SUB, LANES), F32) for _ in range(5)]
        for g in range(GROUP):
            x = half * GROUP + g
            f0 = flat_inc[pl.ds(x, 8, stride=nx), :]
            f1 = flat_inc[pl.ds(8 * nx + x, 8, stride=nx), :]
            a0 = swap_pairs(flat_cot[pl.ds(x, 8, stride=nx), :])
            a1 = swap_first(flat_cot[pl.ds(8 * nx + x, 8, stride=nx), :])
            last = [
                flat_inc[pl.ds(16 * nx + x, 1), :],
                flat_inc[pl.ds(17 * nx + x, 1), :],
                flat_cot[pl.ds(16 * nx + x, 1), :],
                flat_cot[pl.ds(17 * nx + x, 1), :],
                code[x : x + 1],
                ends[x : x + 1],
            ]
            tail = jnp.zeros((SUB, LANES), F32)
            for i, value in enumerate(last):
                tail = jnp.where(row == i, jnp.broadcast_to(value, (SUB, LANES)), tail)
            mine = lane // (2 * HALO) == g
            for i, value in enumerate((f0, f1, a0, a1, tail)):
                edge[i] = jnp.where(mine, roll(value, 2 * HALO * g + HALO, 1), edge[i])
            for i, value in enumerate((f0, f1, shifted(a0), a1, tail)):
                pk[0, x, pl.ds(8 * i, 8), :] = value
                if x < HALO:
                    xl[0, x, pl.ds(8 * i, 8), :] = value
                if x >= nx - HALO:
                    xr[0, x - nx + HALO, pl.ds(8 * i, 8), :] = value
        for i in range(5):
            es[0, half, pl.ds(8 * i, 8), :] = edge[i]


def pack(incident, cotangent, material, lower, upper):
    ports, cz, nx, ny = incident.shape
    halves = nx // GROUP
    field = pl.BlockSpec((ports, 1, nx, ny), lambda z: (0, z, 0, 0))
    codes = pl.BlockSpec((1, nx, material.shape[2]), lambda z: (z, 0, 0))
    ends = pl.BlockSpec((1, nx, material.shape[2]), lambda z: (0, 0, 0))

    def out(rows):
        return pl.BlockSpec((1, rows, MSG, LANES), lambda z: (z, 0, 0, 0))

    def shape(rows):
        return jax.ShapeDtypeStruct((cz, rows, MSG, LANES), F32)

    sizes = (nx, halves, HALO, HALO)
    return pl.pallas_call(
        pack_kernel,
        grid=(cz,),
        in_specs=[field, field, codes, ends, ends],
        out_specs=[out(n) for n in sizes],
        out_shape=[shape(n) for n in sizes],
        compiler_params=pltpu.CompilerParams(vmem_limit_bytes=24 * MIB),
        name="pack",
    )(incident, cotangent, material, lower, upper)


def build_tables(scatter, deriv, tables):
    nmat, ports, _ = scatter.shape
    r = iota((ROWS, ports), 0)
    c = iota((ROWS, ports), 1)
    tail = (r >= 16) & (c == 16 + r % 2)
    natural = (((r < 16) & (r == c)) | tail).astype(F32).astype(BF16)
    swapped_port = jnp.where(r < 12, r + jnp.where(r % 4 < 2, 2, -2), r)
    permuted = (((r < 16) & (swapped_port == c)) | tail).astype(F32).astype(BF16)
    plain = (r == c).astype(F32).astype(BF16)
    q = iota((ports, KDIM), 0)
    k = iota((ports, KDIM), 1)

    def place(m):
        main = (k < 128) & ((k // 16) % 4 == m) & (q == k % 16)
        end = (k >= 128) & ((k % 8) // 2 == m) & (q == 16 + k % 2)
        return (main | end).astype(F32).astype(BF16)

    places = [place(m) for m in range(nmat)]

    def split(value):
        high = value.astype(BF16)
        return high, (value - high.astype(F32)).astype(BF16)

    def form(table, rows, transpose):
        parts = []
        for part in range(2):
            total = jnp.zeros((ROWS, KDIM), F32)
            for m in range(nmat):
                piece = split(table[m])[part]
                axes = (((1,), (1 if transpose else 0,)), ((), ()))
                picked = lax.dot_general(rows, piece, axes, preferred_element_type=F32).astype(BF16)
                total = total + jnp.dot(picked, places[m], preferred_element_type=F32)
            parts.append(total.astype(BF16))
        return parts

    forms = (
        form(scatter, permuted, False)
        + form(deriv, plain, False)
        + form(scatter, permuted, True)
        + form(scatter, natural, True)
    )
    for i, value in enumerate(forms):
        tables[pl.ds(ROWS * i, ROWS), :] = value.astype(F32)


def main_kernel(
    flags, scatter, deriv, pk, fl, fr, hl, hr,
    adjoint, column,
    rf0, rf1, ra0, ra1, rtail, masks, saved_d, saved_r, xf, xa, tf, ta, acc, tables, ebuf, sems,
):
    cz, nx = pk.shape[0], pk.shape[1]
    ne = nx + 2 * HALO
    nb = rf0.shape[1] - ne
    rf, ra = (rf0, rf1), (ra0, ra1)
    row = iota((SUB, LANES), 0)
    lane = iota((SUB, LANES), 1)
    is_first = flags[0] == 1
    is_last = flags[1] == 1

    copies = []
    for i, (source, first, count) in enumerate(((pk, HALO, nx), (hl, 0, HALO), (hr, HALO + nx, HALO))):
        src = source.at[:, pl.ds(0, count)]
        for j, (target, at, size) in enumerate(
            ((rf0.at[:, pl.ds(first, count), pl.ds(0, 16)], 0, 16),
             (ra0.at[:, pl.ds(first, count), pl.ds(0, 16)], 16, 16),
             (rtail.at[:, pl.ds(first, count)], 32, 8))
        ):
            copies.append(pltpu.make_async_copy(src.at[:, :, pl.ds(at, size)], target, sems.at[3 * i + j]))
    for copy in copies:
        copy.start()
    build_tables(scatter, deriv, tables)

    def halo_blocks(z, _):
        for i in range(5):
            part = pl.ds(8 * i, 8)
            blocks = [
                roll(jnp.where(lane % 8 < HALO, fl[z, h, part, :], fr[z, h, part, :]), 8 * HALO, 1)
                for h in range(nb - 1)
            ]
            for b in range(nb):
                before = hl[z, HALO, part, :] if b == 0 else blocks[b - 1]
                after = hr[z, HALO, part, :] if b == nb - 1 else blocks[b]
                value = jnp.where(lane < 8 * HALO, before, after)
                if i == 0 or i == 1:
                    rf0[z, ne + b, part, :] = value
                elif i == 2:
                    ra0[z, ne + b, pl.ds(0, 8), :] = shifted(value)
                elif i == 3:
                    ra0[z, ne + b, pl.ds(8, 8), :] = value
                else:
                    rtail[z, ne + b] = value
        return 0

    lax.fori_loop(0, cz, halo_blocks, 0)
    for copy in copies:
        copy.wait()

    def repeated(value):
        value = jnp.where(row < 2, value, 0.0)
        value = value + roll(value, 2, 0)
        return value + roll(value, 4, 0)

    wide_row = iota((16, LANES), 0)

    def start_rows(r, _):
        for z in range(cz):
            t = rtail[z, r]
            rf0[z, r, pl.ds(16, 8), :] = repeated(t)
            ra0[z, r, pl.ds(16, 8), :] = repeated(roll(t, 6, 0))
            code = jnp.broadcast_to(rtail[z, r, pl.ds(4, 1), :], (16, LANES))
            for m in range(4):
                masks[z, r, pl.ds(16 * m, 16), :] = jnp.where(code == m, 1.0, 0.0).astype(BF16)
            own = ((wide_row % 8) // 2).astype(F32)
            masks[z, r, pl.ds(64, 16), :] = jnp.where(code == own, 1.0, 0.0).astype(BF16)
        return 0

    lax.fori_loop(0, ne + nb, start_rows, 0)

    def operand(values, mask):
        v0, v1, v2 = values
        main = jnp.concatenate([v0, v1], axis=0)
        high = main.astype(BF16)
        low = (main - high.astype(F32)).astype(BF16)
        high2 = v2.astype(BF16).astype(F32)
        end = jnp.concatenate([high2, v2 - high2], axis=0).astype(BF16)
        pieces = [high * mask[m] for m in range(4)] + [low * mask[m] for m in range(4)]
        return jnp.concatenate(pieces + [end * mask[4]], axis=0)

    def mask_of(z, r):
        return [masks[z, r, pl.ds(16 * m, 16), :] for m in range(5)]

    def apply(table, values, mask):
        rhs = jnp.concatenate([operand(values[h], mask[h]) for h in range(2)], axis=1)
        y = jnp.dot(table, rhs, preferred_element_type=F32)
        outs = []
        for h in range(2):
            part = y[:, h * LANES : (h + 1) * LANES]
            outs.append([
                [part[at + 8 * i : at + 8 * i + 8] + part[at + ROWS + 8 * i : at + ROWS + 8 * i + 8] for i in range(3)]
                for at in range(0, table.shape[0], 2 * ROWS)
            ])
        return outs

    def load(ref, z, r, i):
        return ref[z, r, pl.ds(8 * i, 8), :]

    def read(ref, z, r):
        return [load(ref, z, r, i) for i in range(3)]

    def along_z(ref, z, r):
        own = load(ref, z, r, 1)
        if z + 1 < cz:
            above = load(ref, z + 1, r, 1)
        else:
            above = jnp.broadcast_to(rtail[z, r, pl.ds(5, 1), :], (SUB, LANES)) * roll(own, 6, 0)
        if z > 0:
            below = load(ref, z - 1, r, 1)
        else:
            below = jnp.broadcast_to(rtail[z, r, pl.ds(5, 1), :], (SUB, LANES)) * roll(own, 2, 0)
        return jnp.where(row < 2, above, jnp.where(row < 4, below, own))

    at_ends = ((row // 2 == 2) & (lane == LANES - 1)) | ((row // 2 == 3) & (lane == 0))
    at_edges = ((row // 2 == 2) & (lane % 8 == HALO - 1)) | ((row // 2 == 3) & (lane % 8 == HALO))

    def connect_row(ref, tm, z, e):
        amount = LANES - (8 * (e % GROUP) + HALO)
        outer = roll(tm[z, e // GROUP], amount, 1)
        own = jnp.where(at_ends, outer, load(ref, z, e, 0))
        first = jnp.where(row < 2, load(ref, z, e + 1, 0), jnp.where(row < 4, load(ref, z, e - 1, 0), own))
        return [first, along_z(ref, z, e), load(ref, z, e, 2)]

    def connect_edge(ref, x, tm, z, b):
        own = load(ref, z, ne + b, 0)
        nxt = load(ref, z, ne + (b + 1) % nb, 0)
        prv = load(ref, z, ne + (b + nb - 1) % nb, 0)
        after = roll(jnp.where(lane >= 8, own, nxt), LANES - 8, 1)
        before = roll(jnp.where(lane < LANES - 8, own, prv), 8, 1)
        inner = x[z, b]
        top = roll(roll(inner, LANES - 1, 1), 6, 0)
        bottom = roll(roll(inner, 1, 1), 2, 0)
        tm[z, b] = jnp.where(is_last & (row < 6), -top, jnp.where(is_first & (row >= 6), -bottom, own))
        own = jnp.where(at_edges, inner, own)
        first = jnp.where(row < 2, after, jnp.where(row < 4, before, own))
        return [first, along_z(ref, z, ne + b), load(ref, z, ne + b, 2)]

    def collect(x, z, e, block):
        g = e % GROUP
        moved = roll(block, 8 * g + HALO, 1)
        x[z, e // GROUP] = jnp.where(lane // 8 == g, moved, x[z, e // GROUP])

    def write(ref, z, r, part):
        first = shifted(part[0])
        ref[z, r, pl.ds(0, 8), :] = first
        ref[z, r, pl.ds(8, 8), :] = part[1]
        ref[z, r, pl.ds(16, 8), :] = part[2]
        return first

    for x in (xf, xa):
        x[...] = jnp.zeros_like(x)

    def gather_first(e, _):
        for z in range(cz):
            collect(xa, z, e, ra0[z, e, pl.ds(0, 8), :])
        return 0

    lax.fori_loop(0, ne, gather_first, 0, unroll=2)
    flat = adjoint.reshape(adjoint.shape[0] * cz * nx, LANES)

    def in_pairs(before, after):
        pending = None
        for z in range(0, cz, 2):
            made = before(z)
            if pending is not None:
                after(*pending)
            pending = (z, made)
        after(*pending)

    for step in range(ITERS):
        fa, ta_, fb, tb = rf[step % 2], ra[step % 2], rf[(step + 1) % 2], ra[(step + 1) % 2]
        last = step == ITERS - 1
        a_table = tables[pl.ds((6 if last else 4) * ROWS, 2 * ROWS), :].astype(BF16)
        if last:
            f_table = tables[pl.ds(2 * ROWS, 2 * ROWS), :].astype(BF16)
        else:
            f_table = tables[pl.ds(0, 4 * ROWS), :].astype(BF16)
        s_table = tables[pl.ds(0, 2 * ROWS), :].astype(BF16)

        for b in range(nb):
            def before(z, b=b):
                av = [connect_edge(ta_, xa, ta, z + h, b) for h in range(2)]
                if step > 0:
                    fv = [connect_edge(fa, xf, tf, z + h, b) for h in range(2)]
                else:
                    fv = [read(fa, z + h, ne + b) for h in range(2)]
                if last:
                    return None
                mask = [mask_of(z + h, ne + b) for h in range(2)]
                return apply(a_table, av, mask), apply(s_table, fv, mask)

            def after(z, made, b=b):
                if last:
                    return
                for h in range(2):
                    write(tb, z + h, ne + b, made[0][h][0])
                    write(fb, z + h, ne + b, made[1][h][0])

            in_pairs(before, after)

        def rows(e, _):
            total = []

            def before(z):
                mask = [mask_of(z + h, e) for h in range(2)]
                av = [connect_row(ta_, ta, z + h, e) for h in range(2)]
                a_out = apply(a_table, av, mask)
                if step < 2:
                    for h in range(2):
                        for i in range(3):
                            saved_r[step, z + h, e, pl.ds(8 * i, 8), :] = av[h][i]
                else:
                    for h in range(2):
                        for i in range(3):
                            total.append(av[h][i] * load(saved_d.at[ITERS - 1 - step], z + h, e, i))
                if step > 0:
                    fv = [connect_row(fa, tf, z + h, e) for h in range(2)]
                else:
                    fv = [read(fa, z + h, e) for h in range(2)]
                return a_out, apply(f_table, fv, mask)

            def after(z, made):
                a_out, f_out = made
                for h in range(2):
                    part = a_out[h][0]
                    if last:
                        at = (z + h) * nx + e - HALO
                        flat[pl.ds(at, 8, stride=cz * nx), :] = part[0]
                        flat[pl.ds(8 * cz * nx + at, 8, stride=cz * nx), :] = part[1]
                        flat[pl.ds(16 * cz * nx + at, 1), :] = part[2][0:1]
                        flat[pl.ds(17 * cz * nx + at, 1), :] = part[2][1:2]
                        change = f_out[h][0]
                    else:
                        collect(xa, z + h, e, write(tb, z + h, e, part))
                        collect(xf, z + h, e, write(fb, z + h, e, f_out[h][0]))
                        change = f_out[h][1]
                    for i in range(3):
                        if step < 2:
                            saved_d[step, z + h, e, pl.ds(8 * i, 8), :] = change[i]
                        else:
                            total.append(change[i] * load(saved_r.at[ITERS - 1 - step], z + h, e, i))
                if total:
                    value = functools.reduce(lambda p, q: p + q, total)
                    del total[:]
                    total.append(value)

            in_pairs(before, after)
            if step == 2:
                acc[e] = total[0]
            elif step > 2:
                acc[e] = acc[e] + total[0]
            return 0

        first, end = 1 + step, ne - 1 - step
        spare = (end - first) % CHUNK
        for e in range(first, first + spare):
            rows(e, 0)

        def chunk(c, _):
            for i in range(CHUNK):
                rows(first + spare + c * CHUNK + i, 0)
            return 0

        lax.fori_loop(0, (end - first) // CHUNK, chunk, 0)

    for x in range(nx):
        column[pl.ds(x, 1), :] = jnp.sum(acc[HALO + x], axis=0, keepdims=True) * sens_scale


def main_call(flags, scatter, deriv, pk, fl, fr, hl, hr):
    cz, nx = pk.shape[0], pk.shape[1]
    ports = scatter.shape[1]
    ne = nx + 2 * HALO
    nb = ne // GROUP + 1
    total = ne + nb
    return pl.pallas_call(
        main_kernel,
        in_specs=[SMEM, VMEM, VMEM, ANY, VMEM, VMEM, VMEM, VMEM],
        out_specs=[VMEM, VMEM],
        out_shape=[
            jax.ShapeDtypeStruct((ports, cz, nx, LANES), F32),
            jax.ShapeDtypeStruct((nx, LANES), F32),
        ],
        scratch_shapes=[
            pltpu.VMEM((cz, total, ROWS, LANES), F32),
            pltpu.VMEM((cz, total, ROWS, LANES), F32),
            pltpu.VMEM((cz, total, ROWS, LANES), F32),
            pltpu.VMEM((cz, total, ROWS, LANES), F32),
            pltpu.VMEM((cz, total, SUB, LANES), F32),
            pltpu.VMEM((cz, total, 80, LANES), BF16),
            pltpu.VMEM((2, cz, ne, ROWS, LANES), F32),
            pltpu.VMEM((2, cz, ne, ROWS, LANES), F32),
            pltpu.VMEM((cz, nb, SUB, LANES), F32),
            pltpu.VMEM((cz, nb, SUB, LANES), F32),
            pltpu.VMEM((cz, nb, SUB, LANES), F32),
            pltpu.VMEM((cz, nb, SUB, LANES), F32),
            pltpu.VMEM((ne, SUB, LANES), F32),
            pltpu.VMEM((8 * ROWS, KDIM), F32),
            pltpu.VMEM((SUB, LANES), F32),
            pltpu.SemaphoreType.DMA((9,)),
        ],
        compiler_params=pltpu.CompilerParams(vmem_limit_bytes=63 * MIB),
        name="adjoint_steps",
    )(flags, scatter, deriv, pk, fl, fr, hl, hr)


def route_kernel(ids, owner_hot, rank_hot, id_slots):
    nx = ids.shape[0]
    ndev, cap = id_slots.shape
    owned = nx * LANES
    who = iota((ndev, LANES), 0)
    place = iota((cap, LANES), 0)
    before = (iota((LANES, LANES), 0) < iota((LANES, LANES), 1)).astype(BF16)
    offset = jnp.zeros((ndev, 1), F32)
    id_slots[...] = jnp.zeros_like(id_slots)
    for x in range(nx):
        wanted = ids[pl.ds(x, 1), :]
        hot = (wanted // owned == who).astype(F32)
        counts = jnp.dot(hot.astype(BF16), before, preferred_element_type=F32) + offset
        rank = jnp.sum(hot * counts, axis=0, keepdims=True).astype(jnp.int32)
        ranked = (rank == place).astype(F32).astype(BF16)
        offset = offset + jnp.sum(hot, axis=1, keepdims=True)
        local = wanted % owned
        owner_hot[:, pl.ds(x * LANES, LANES)] = hot.astype(BF16)
        rank_hot[:, pl.ds(x * LANES, LANES)] = ranked
        high = (hot * (local // 64).astype(F32)).astype(BF16)
        low = (hot * (local % 64).astype(F32)).astype(BF16)
        both = lax.dot_general(
            jnp.concatenate([high, low], axis=0), ranked, (((1,), (1,)), ((), ())), preferred_element_type=F32
        )
        id_slots[...] += 64.0 * both[:ndev] + both[ndev:]


def route(ids, ndev, cap):
    n = ids.shape[0] * ids.shape[1]
    return pl.pallas_call(
        route_kernel,
        in_specs=[VMEM],
        out_specs=[VMEM] * 3,
        out_shape=[
            jax.ShapeDtypeStruct((ndev, n), BF16),
            jax.ShapeDtypeStruct((cap, n), BF16),
            jax.ShapeDtypeStruct((ndev, cap), F32),
        ],
        compiler_params=pltpu.CompilerParams(vmem_limit_bytes=24 * MIB),
        name="route",
    )(ids)


def send_kernel(column, owner_hot, rank_hot, id_slots, message):
    nx = column.shape[0]
    ndev, cap = id_slots.shape
    total = jnp.zeros((2 * ndev, cap), F32)
    for x in range(nx):
        value = jnp.broadcast_to(column[pl.ds(x, 1), :], (ndev, LANES))
        high = value.astype(BF16)
        low = (value - high.astype(F32)).astype(BF16)
        part = pl.ds(x * LANES, LANES)
        hot = owner_hot[:, part]
        total = total + lax.dot_general(
            jnp.concatenate([high * hot, low * hot], axis=0), rank_hot[:, part],
            (((1,), (1,)), ((), ())), preferred_element_type=F32,
        )
    message[:, pl.ds(0, cap)] = total[:ndev] + total[ndev:]
    message[:, pl.ds(cap, cap)] = id_slots[...]


def send(column, owner_hot, rank_hot, id_slots):
    ndev, cap = id_slots.shape
    return pl.pallas_call(
        send_kernel,
        in_specs=[VMEM] * 4,
        out_specs=VMEM,
        out_shape=jax.ShapeDtypeStruct((ndev, 2 * cap), F32),
        compiler_params=pltpu.CompilerParams(vmem_limit_bytes=24 * MIB),
        name="send",
    )(column, owner_hot, rank_hot, id_slots)


def gather_kernel(message, out):
    ndev, cap = message.shape[0], message.shape[1] // 2
    nrow = out.shape[0]
    rows = iota((nrow, cap), 0)
    lanes = iota((LANES, cap), 0)
    total = jnp.zeros((2 * nrow, LANES), F32)
    for s in range(ndev):
        value = jnp.broadcast_to(message[pl.ds(s, 1), pl.ds(0, cap)], (nrow, cap))
        local = message[pl.ds(s, 1), pl.ds(cap, cap)].astype(jnp.int32)
        high = value.astype(BF16).astype(F32)
        mine = local // LANES == rows
        left = jnp.concatenate([jnp.where(mine, high, 0.0), jnp.where(mine, value - high, 0.0)], axis=0)
        right = (local % LANES == lanes).astype(F32).astype(BF16)
        total = total + lax.dot_general(
            left.astype(BF16), right, (((1,), (1,)), ((), ())), preferred_element_type=F32
        )
    out[...] = total[:nrow] + total[nrow:]


def gather(message, owned):
    return pl.pallas_call(
        gather_kernel,
        in_specs=[VMEM],
        out_specs=VMEM,
        out_shape=jax.ShapeDtypeStruct((owned // LANES, LANES), F32),
        compiler_params=pltpu.CompilerParams(vmem_limit_bytes=24 * MIB),
        name="gather",
    )(message)


def moved(block, axis, distance, wrap):
    count = lax.axis_size(axis)
    pairs = [(i, (i + distance) % count) for i in range(count) if wrap or 0 <= i + distance < count]
    return lax.ppermute(block, axis, pairs)


def shards(incident, cotangent, scatter_table, deriv_table, material_code, boundary_code, param_ids):
    position = lax.axis_index("gy")
    extent = lax.axis_size("gy")
    ndev = lax.axis_size("gx") * extent
    owned = param_ids.shape[0] * param_ids.shape[1]
    cap = 2 * owned // ndev
    pk, es, xl, xr = pack(incident, cotangent, material_code, boundary_code[0:1], boundary_code[1:2])
    fl = moved(es, "gy", 1, False)
    fr = moved(es, "gy", -1, False)
    owner_hot, rank_hot, id_slots = route(param_ids, ndev, cap)
    near = (jnp.arange(LANES) % (2 * HALO) < HALO)[None, None, None]
    low = jnp.where(near, fl[:, :1], fr[:, :1])
    high = jnp.where(near, fl[:, -1:], fr[:, -1:])
    place = 8 * HALO
    low = jnp.roll(low, place, axis=3)
    high = jnp.roll(high, place, axis=3)
    hr = moved(jnp.concatenate([xl, low], axis=1), "gx", -1, True)
    hl = moved(jnp.concatenate([xr, high], axis=1), "gx", 1, True)
    flags = jnp.stack([position == 0, position == extent - 1]).astype(jnp.int32)
    adjoint, column = main_call(flags, scatter_table, deriv_table, pk, fl, fr, hl, hr)
    message = send(column, owner_hot, rank_hot, id_slots)
    received = lax.all_to_all(message, ("gx", "gy"), 0, 0, tiled=True)
    sensitivity = gather(received, owned).reshape(-1)
    return adjoint, sensitivity


def solution(mesh):
    in_specs = (
        P(None, None, "gx", "gy"),
        P(None, None, "gx", "gy"),
        P(),
        P(),
        P(None, "gx", "gy"),
        P(None, "gx", "gy"),
        P("gx", "gy"),
    )
    out_specs = (P(None, None, "gx", "gy"), P(("gx", "gy")))
    return jax.shard_map(shards, mesh=mesh, in_specs=in_specs, out_specs=out_specs, check_vma=False)
```

```python
import functools

import jax
import jax.numpy as jnp
from jax import lax
from jax.experimental import pallas as pl
from jax.experimental.pallas import tpu as pltpu
from jax.sharding import PartitionSpec as P

BW = 8
ITERS = 4
CHUNK = 8
PACK_VMEM = 60
HALO = 4
SUB = 8
LANES = 128
GROUP = LANES // (2 * HALO)
MSG = 40
DEEP = 3
ROWS = 24
KDIM = 144
F32 = jnp.float32
BF16 = jnp.bfloat16
sens_scale = 1.0 / 32.0
MIB = 2**20
VMEM = pl.BlockSpec(memory_space=pltpu.VMEM)
SMEM = pl.BlockSpec(memory_space=pltpu.SMEM)
ANY = pl.BlockSpec(memory_space=pl.ANY)


def iota(shape, dim):
    return lax.broadcasted_iota(jnp.int32, shape, dim)


def roll(value, amount, axis):
    return pltpu.roll(value, amount, axis)


def shifted(block):
    row = iota((SUB, LANES), 0)
    up = roll(block, LANES - 1, 1)
    down = roll(block, 1, 1)
    return jnp.where(row < 4, block, jnp.where(row < 6, up, down))


def swap_pairs(block):
    row = iota((SUB, LANES), 0)
    return jnp.where(row % 4 < 2, roll(block, SUB - 2, 0), roll(block, 2, 0))


def swap_first(block):
    row = iota((SUB, LANES), 0)
    return jnp.where(row < 4, swap_pairs(block), block)


def near_lanes(first):
    lane = iota((SUB, LANES), 1)
    x = jnp.clip(first + lane // (2 * HALO), 0, LANES // HALO - 1)
    c = lane % HALO
    return HALO * x + c, HALO * ((x + 1) % (LANES // HALO)) + c


def pick(below, above, lanes):
    lane = iota((SUB, LANES), 1)
    below = jnp.take_along_axis(below, lanes[0], axis=1)
    above = jnp.take_along_axis(above, lanes[1], axis=1)
    return jnp.where(lane % (2 * HALO) < HALO, below, above)


def pack_kernel(inc, cot, mat, ends, pk, up, down, xl, xr):
    z = pl.program_id(0)
    cz = pl.num_programs(0)
    nx = inc.shape[2]
    lane = iota((SUB, LANES), 1)
    row = iota((SUB, LANES), 0)
    width = mat.shape[1]
    spread = (iota((width, LANES), 1) // BW == iota((width, LANES), 0)).astype(F32).astype(BF16)

    def expand(codes):
        dims = (((0,), (0,)), ((), ()))
        return lax.dot_general(codes.astype(F32).astype(BF16), spread, dims, preferred_element_type=F32)

    def coefficient(codes):
        return jnp.where(codes == 0, -1.0, jnp.where(codes == 1, 1.0, 0.0))

    code = expand(mat[0])
    lower = expand(coefficient(ends[0]))
    upper = expand(coefficient(ends[1]))
    end = jnp.where(z == 0, lower, jnp.where(z == cz - 1, upper, 0.0))
    flat_inc = inc.reshape(inc.shape[0] * nx, LANES)
    flat_cot = cot.reshape(cot.shape[0] * nx, LANES)
    to_up = [jnp.zeros((SUB, LANES), F32) for _ in range(5)]
    to_down = [jnp.zeros((SUB, LANES), F32) for _ in range(5)]
    firsts = {}
    for x in range(nx):
        f0 = flat_inc[pl.ds(x, 8, stride=nx), :]
        f1 = flat_inc[pl.ds(8 * nx + x, 8, stride=nx), :]
        a0 = swap_pairs(flat_cot[pl.ds(x, 8, stride=nx), :])
        a1 = swap_first(flat_cot[pl.ds(8 * nx + x, 8, stride=nx), :])
        last = [
            flat_inc[pl.ds(16 * nx + x, 1), :],
            flat_inc[pl.ds(17 * nx + x, 1), :],
            flat_cot[pl.ds(16 * nx + x, 1), :],
            flat_cot[pl.ds(17 * nx + x, 1), :],
            code[x : x + 1],
            end[x : x + 1],
        ]
        tail = jnp.zeros((SUB, LANES), F32)
        for i, value in enumerate(last):
            tail = jnp.where(row == i, jnp.broadcast_to(value, (SUB, LANES)), tail)
        group = lane // HALO
        for i, value in enumerate((f0, f1, a0, a1, tail)):
            turned = roll(value, (HALO * x + HALO) % LANES, 1) if x + 1 < nx else value
            to_up[i] = jnp.where(group == x, turned, to_up[i])
            to_down[i] = jnp.where(group == (x + 1) % nx, turned, to_down[i])
        firsts[x] = a0
        for i, value in enumerate((f0, f1, shifted(a0), a1, tail)):
            pk[0, x, pl.ds(8 * i, 8), :] = value
            if x < DEEP:
                xl[0, pl.ds(MSG * x + 8 * i, 8), :] = value
            if x >= nx - DEEP:
                xr[0, pl.ds(MSG * (x - nx + DEEP) + 8 * i, 8), :] = value
    xl[0, pl.ds(DEEP * MSG - 2, 2), :] = firsts[DEEP][0:2]
    xr[0, pl.ds(MSG - 2, 2), :] = firsts[nx - DEEP - 1][2:4]
    for i in range(5):
        up[0, pl.ds(8 * i, 8), :] = to_up[i]
        down[0, pl.ds(8 * i, 8), :] = to_down[i]


def pack(incident, cotangent, material, ends):
    ports, cz, nx, ny = incident.shape
    field = pl.BlockSpec((ports, 1, nx, ny), lambda z: (0, z, 0, 0))
    codes = pl.BlockSpec((1,) + material.shape[1:], lambda z: (z, 0, 0))
    both = pl.BlockSpec(ends.shape, lambda z: (0, 0, 0))
    edge = pl.BlockSpec((1, MSG, LANES), lambda z: (z, 0, 0))
    deep = pl.BlockSpec((1, DEEP * MSG, LANES), lambda z: (z, 0, 0))
    return pl.pallas_call(
        pack_kernel,
        grid=(cz,),
        in_specs=[field, field, codes, both],
        out_specs=[pl.BlockSpec((1, nx, MSG, LANES), lambda z: (z, 0, 0, 0)), edge, edge, deep, deep],
        out_shape=[
            jax.ShapeDtypeStruct((cz, nx, MSG, LANES), F32),
            jax.ShapeDtypeStruct((cz, MSG, LANES), F32),
            jax.ShapeDtypeStruct((cz, MSG, LANES), F32),
            jax.ShapeDtypeStruct((cz + 1, DEEP * MSG, LANES), F32),
            jax.ShapeDtypeStruct((cz + 1, DEEP * MSG, LANES), F32),
        ],
        compiler_params=pltpu.CompilerParams(vmem_limit_bytes=PACK_VMEM * MIB),
        name="pack",
    )(incident, cotangent, material, ends)


def corner_kernel(below, above, xl_in, xr_in, xl, xr, left, right, sems):
    cz = below.shape[0]
    nx = LANES // HALO
    lane = iota((SUB, LANES), 1)
    x = (lane % 32) // (2 * HALO)
    c = lane % HALO

    def lanes(first):
        return HALO * (first + x) + c, HALO * ((first + x + 1) % nx) + c

    low, high = lanes(0), lanes(nx - HALO)
    for out, place in ((left, low), (right, high)):
        for q in range(DEEP):
            for i in range(5):
                part = pl.ds(8 * i, 8)
                value = jnp.zeros((SUB, LANES), F32)
                for h in range(4):
                    z = 4 * q + h
                    if z < cz:
                        value = jnp.where(lane // 32 == h, pick(below[z, part, :], above[z, part, :], place), value)
                out[pl.ds(MSG * q + 8 * i, 8), :] = value
    copies = [
        pltpu.make_async_copy(left, xl.at[cz], sems.at[0]),
        pltpu.make_async_copy(right, xr.at[cz], sems.at[1]),
    ]
    for copy in copies:
        copy.start()
    for copy in copies:
        copy.wait()


def corners(below, above, xl, xr):
    shape = jax.ShapeDtypeStruct(xl.shape, F32)
    return pl.pallas_call(
        corner_kernel,
        in_specs=[VMEM, VMEM, ANY, ANY],
        out_specs=[ANY, ANY],
        out_shape=[shape, shape],
        input_output_aliases={2: 0, 3: 1},
        scratch_shapes=[
            pltpu.VMEM((DEEP * MSG, LANES), F32),
            pltpu.VMEM((DEEP * MSG, LANES), F32),
            pltpu.SemaphoreType.DMA((2,)),
        ],
        compiler_params=pltpu.CompilerParams(vmem_limit_bytes=16 * MIB),
        name="corners",
    )(below, above, xl, xr)


def build_tables(scatter, deriv, tables):
    nmat, ports, _ = scatter.shape
    r = iota((ROWS, ports), 0)
    c = iota((ROWS, ports), 1)
    tail = (r >= 16) & (c == 16 + r % 2)
    natural = (((r < 16) & (r == c)) | tail).astype(F32).astype(BF16)
    swapped_port = jnp.where(r < 12, r + jnp.where(r % 4 < 2, 2, -2), r)
    permuted = (((r < 16) & (swapped_port == c)) | tail).astype(F32).astype(BF16)
    plain = (r == c).astype(F32).astype(BF16)
    q = iota((ports, KDIM), 0)
    k = iota((ports, KDIM), 1)

    def place(m):
        main = (k < 128) & ((k // 16) % 4 == m) & (q == k % 16)
        end = (k >= 128) & ((k % 8) // 2 == m) & (q == 16 + k % 2)
        return (main | end).astype(F32).astype(BF16)

    places = [place(m) for m in range(nmat)]

    def split(value):
        high = value.astype(BF16)
        return high, (value - high.astype(F32)).astype(BF16)

    def form(table, rows, transpose):
        parts = []
        for part in range(2):
            total = jnp.zeros((ROWS, KDIM), F32)
            for m in range(nmat):
                piece = split(table[m])[part]
                axes = (((1,), (1 if transpose else 0,)), ((), ()))
                picked = lax.dot_general(rows, piece, axes, preferred_element_type=F32).astype(BF16)
                total = total + jnp.dot(picked, places[m], preferred_element_type=F32)
            parts.append(total.astype(BF16))
        return parts

    forms = (
        form(scatter, permuted, False)
        + form(deriv, plain, False)
        + form(scatter, permuted, True)
        + form(scatter, natural, True)
    )
    for i, value in enumerate(forms):
        tables[pl.ds(ROWS * i, ROWS), :] = value.astype(F32)


def main_kernel(
    flags, scatter, deriv, pk, fl, fr, hl, hr,
    adjoint, column,
    rf0, rf1, ra0, ra1, rtail, masks, saved_d, saved_r, xf, xa, tf, ta, acc, tables, cbuf, sems,
):
    cz, nx = pk.shape[0], pk.shape[1]
    ne = nx + 2 * HALO
    nb = rf0.shape[1] - ne
    rf, ra = (rf0, rf1), (ra0, ra1)
    row = iota((SUB, LANES), 0)
    lane = iota((SUB, LANES), 1)
    is_first = flags[0] == 1
    is_last = flags[1] == 1

    copies = []

    def bring(source, target):
        copies.append(pltpu.make_async_copy(source, target, sems.at[len(copies)]))

    for buffer, at in ((rf0, 0), (ra0, 16)):
        bring(pk.at[:, :, pl.ds(at, 16)], buffer.at[:, pl.ds(HALO, nx), pl.ds(0, 16)])
    bring(pk.at[:, :, pl.ds(32, 8)], rtail.at[:, pl.ds(HALO, nx)])
    for source, first in ((hl, HALO - DEEP), (hr, HALO + nx)):
        for i in range(DEEP):
            for buffer, at in ((rf0, 0), (ra0, 16)):
                bring(source.at[pl.ds(0, cz), pl.ds(MSG * i + at, 16)], buffer.at[:, first + i, pl.ds(0, 16)])
            bring(source.at[pl.ds(0, cz), pl.ds(MSG * i + 32, 8)], rtail.at[:, first + i])
    for q in range(DEEP):
        for i, source in enumerate((hl, hr)):
            bring(source.at[cz, pl.ds(MSG * q, MSG)], cbuf.at[i, q])
    for copy in copies:
        copy.start()
    build_tables(scatter, deriv, tables)
    for copy in copies:
        copy.wait()

    places = [near_lanes(GROUP * b - HALO) for b in range(nb)]

    def halo_blocks(z, _):
        turn = LANES - 32 * (z % 4)
        for i in range(5):
            part = pl.ds(8 * i, 8)
            for b in range(nb):
                value = pick(fl[z, part, :], fr[z, part, :], places[b])
                if b == 0:
                    outer = roll(cbuf[0, z // 4, part, :], turn % LANES, 1)
                    value = jnp.where(lane < 8 * HALO, outer, value)
                if b == nb - 1:
                    outer = roll(cbuf[1, z // 4, part, :], (turn + 32) % LANES, 1)
                    value = jnp.where(lane < 8 * HALO, value, outer)
                if i == 0 or i == 1:
                    rf0[z, ne + b, part, :] = value
                elif i == 2:
                    ra0[z, ne + b, pl.ds(0, 8), :] = shifted(value)
                elif i == 3:
                    ra0[z, ne + b, pl.ds(8, 8), :] = value
                else:
                    rtail[z, ne + b] = value
        ra0[z, 0, pl.ds(0, 8), :] = roll(rtail[z, HALO - DEEP], 4, 0)
        ra0[z, ne - 1, pl.ds(0, 8), :] = roll(rtail[z, ne - 1 - (HALO - DEEP)], 2, 0)
        return 0

    lax.fori_loop(0, cz, halo_blocks, 0, unroll=2)

    def repeated(value):
        value = jnp.where(row < 2, value, 0.0)
        value = value + roll(value, 2, 0)
        return value + roll(value, 4, 0)

    wide_row = iota((16, LANES), 0)
    own_code = ((wide_row % 8) // 2).astype(F32)

    def start_row(r, _):
        for z in range(cz):
            t = rtail[z, r]
            rf0[z, r, pl.ds(16, 8), :] = repeated(t)
            ra0[z, r, pl.ds(16, 8), :] = repeated(roll(t, 6, 0))
            code = jnp.broadcast_to(rtail[z, r, pl.ds(4, 1), :], (16, LANES))
            for m in range(4):
                masks[z, r, pl.ds(16 * m, 16), :] = jnp.where(code == m, 1.0, 0.0).astype(BF16)
            masks[z, r, pl.ds(64, 16), :] = jnp.where(code == own_code, 1.0, 0.0).astype(BF16)
        return 0

    for b in range(nb):
        start_row(ne + b, 0)
    lax.fori_loop(0, ne // 4, lambda c, _: [start_row(4 * c + i, 0) for i in range(4)][0], 0)

    def operand(values, mask):
        v0, v1, v2 = values
        main = jnp.concatenate([v0, v1], axis=0)
        high = main.astype(BF16)
        low = (main - high.astype(F32)).astype(BF16)
        high2 = v2.astype(BF16).astype(F32)
        end = jnp.concatenate([high2, v2 - high2], axis=0).astype(BF16)
        pieces = [high * mask[m] for m in range(4)] + [low * mask[m] for m in range(4)]
        return jnp.concatenate(pieces + [end * mask[4]], axis=0)

    def mask_of(z, r):
        return [masks[z, r, pl.ds(16 * m, 16), :] for m in range(5)]

    def apply(table, values, mask):
        rhs = jnp.concatenate([operand(values[h], mask[h]) for h in range(2)], axis=1)
        y = jnp.dot(table, rhs, preferred_element_type=F32)
        outs = []
        for h in range(2):
            part = y[:, h * LANES : (h + 1) * LANES]
            outs.append([
                [part[at + 8 * i : at + 8 * i + 8] + part[at + ROWS + 8 * i : at + ROWS + 8 * i + 8] for i in range(3)]
                for at in range(0, table.shape[0], 2 * ROWS)
            ])
        return outs

    def load(ref, z, r, i):
        return ref[z, r, pl.ds(8 * i, 8), :]

    def read(ref, z, r):
        return [load(ref, z, r, i) for i in range(3)]

    def along_z(ref, z, r):
        own = load(ref, z, r, 1)
        if z + 1 < cz:
            above = load(ref, z + 1, r, 1)
        else:
            above = jnp.broadcast_to(rtail[z, r, pl.ds(5, 1), :], (SUB, LANES)) * roll(own, 6, 0)
        if z > 0:
            below = load(ref, z - 1, r, 1)
        else:
            below = jnp.broadcast_to(rtail[z, r, pl.ds(5, 1), :], (SUB, LANES)) * roll(own, 2, 0)
        return jnp.where(row < 2, above, jnp.where(row < 4, below, own))

    at_ends = ((row // 2 == 2) & (lane == LANES - 1)) | ((row // 2 == 3) & (lane == 0))
    at_edges = ((row // 2 == 2) & (lane % 8 == HALO - 1)) | ((row // 2 == 3) & (lane % 8 == HALO))

    def connect_row(ref, tm, z, e):
        amount = LANES - (8 * (e % GROUP) + HALO)
        outer = roll(tm[z, e // GROUP], amount, 1)
        own = jnp.where(at_ends, outer, load(ref, z, e, 0))
        first = jnp.where(row < 2, load(ref, z, e + 1, 0), jnp.where(row < 4, load(ref, z, e - 1, 0), own))
        return [first, along_z(ref, z, e), load(ref, z, e, 2)]

    def connect_edge(ref, x, tm, z, b):
        own = load(ref, z, ne + b, 0)
        nxt = load(ref, z, ne + (b + 1) % nb, 0)
        prv = load(ref, z, ne + (b + nb - 1) % nb, 0)
        after = roll(jnp.where(lane >= 8, own, nxt), LANES - 8, 1)
        before = roll(jnp.where(lane < LANES - 8, own, prv), 8, 1)
        inner = x[z, b]
        top = roll(roll(inner, LANES - 1, 1), 6, 0)
        bottom = roll(roll(inner, 1, 1), 2, 0)
        tm[z, b] = jnp.where(is_last & (row < 6), -top, jnp.where(is_first & (row >= 6), -bottom, own))
        own = jnp.where(at_edges, inner, own)
        first = jnp.where(row < 2, after, jnp.where(row < 4, before, own))
        return [first, along_z(ref, z, ne + b), load(ref, z, ne + b, 2)]

    def collect(x, z, e, block):
        g = e % GROUP
        moved = roll(block, 8 * g + HALO, 1)
        x[z, e // GROUP] = jnp.where(lane // 8 == g, moved, x[z, e // GROUP])

    def write(ref, z, r, part):
        first = shifted(part[0])
        ref[z, r, pl.ds(0, 8), :] = first
        ref[z, r, pl.ds(8, 8), :] = part[1]
        ref[z, r, pl.ds(16, 8), :] = part[2]
        return first

    for x in (xf, xa):
        x[...] = jnp.zeros_like(x)

    def gather_first(e, _):
        for z in range(cz):
            collect(xa, z, e, ra0[z, e, pl.ds(0, 8), :])
        return 0

    lax.fori_loop(0, ne // 4, lambda c, _: [gather_first(4 * c + i, 0) for i in range(4)][0], 0)
    flat = adjoint.reshape(adjoint.shape[0] * cz * nx, LANES)

    def in_pairs(before, after):
        pending = None
        for z in range(0, cz, 2):
            made = before(z)
            if pending is not None:
                after(*pending)
            pending = (z, made)
        after(*pending)

    for step in range(ITERS):
        fa, ta_, fb, tb = rf[step % 2], ra[step % 2], rf[(step + 1) % 2], ra[(step + 1) % 2]
        last = step == ITERS - 1
        a_table = tables[pl.ds((6 if last else 4) * ROWS, 2 * ROWS), :].astype(BF16)
        if last:
            f_table = tables[pl.ds(2 * ROWS, 2 * ROWS), :].astype(BF16)
        else:
            f_table = tables[pl.ds(0, 4 * ROWS), :].astype(BF16)
        s_table = tables[pl.ds(0, 2 * ROWS), :].astype(BF16)

        for b in range(nb):
            def before(z, b=b):
                av = [connect_edge(ta_, xa, ta, z + h, b) for h in range(2)]
                if step > 0:
                    fv = [connect_edge(fa, xf, tf, z + h, b) for h in range(2)]
                else:
                    fv = [read(fa, z + h, ne + b) for h in range(2)]
                if last:
                    return None
                mask = [mask_of(z + h, ne + b) for h in range(2)]
                return apply(a_table, av, mask), apply(s_table, fv, mask)

            def after(z, made, b=b):
                if last:
                    return
                for h in range(2):
                    write(tb, z + h, ne + b, made[0][h][0])
                    write(fb, z + h, ne + b, made[1][h][0])

            in_pairs(before, after)

        def rows(e, _):
            total = []

            def before(z):
                mask = [mask_of(z + h, e) for h in range(2)]
                av = [connect_row(ta_, ta, z + h, e) for h in range(2)]
                a_out = apply(a_table, av, mask)
                if step < 2:
                    for h in range(2):
                        for i in range(3):
                            saved_r[step, z + h, e, pl.ds(8 * i, 8), :] = av[h][i]
                else:
                    for h in range(2):
                        for i in range(3):
                            total.append(av[h][i] * load(saved_d.at[ITERS - 1 - step], z + h, e, i))
                if step > 0:
                    fv = [connect_row(fa, tf, z + h, e) for h in range(2)]
                else:
                    fv = [read(fa, z + h, e) for h in range(2)]
                return a_out, apply(f_table, fv, mask)

            def after(z, made):
                a_out, f_out = made
                for h in range(2):
                    part = a_out[h][0]
                    if last:
                        at = (z + h) * nx + e - HALO
                        flat[pl.ds(at, 8, stride=cz * nx), :] = part[0]
                        flat[pl.ds(8 * cz * nx + at, 8, stride=cz * nx), :] = part[1]
                        flat[pl.ds(16 * cz * nx + at, 1), :] = part[2][0:1]
                        flat[pl.ds(17 * cz * nx + at, 1), :] = part[2][1:2]
                        change = f_out[h][0]
                    else:
                        collect(xa, z + h, e, write(tb, z + h, e, part))
                        collect(xf, z + h, e, write(fb, z + h, e, f_out[h][0]))
                        change = f_out[h][1]
                    for i in range(3):
                        if step < 2:
                            saved_d[step, z + h, e, pl.ds(8 * i, 8), :] = change[i]
                        else:
                            total.append(change[i] * load(saved_r.at[ITERS - 1 - step], z + h, e, i))
                if total:
                    value = functools.reduce(lambda p, q: p + q, total)
                    del total[:]
                    total.append(value)

            in_pairs(before, after)
            if step == 2:
                acc[e] = total[0]
            elif step > 2:
                acc[e] = acc[e] + total[0]
            return 0

        first, end = 1 + step, ne - 1 - step
        spare = (end - first) % CHUNK
        for e in range(first, first + spare):
            rows(e, 0)

        def chunk(c, _):
            for i in range(CHUNK):
                rows(first + spare + c * CHUNK + i, 0)
            return 0

        lax.fori_loop(0, (end - first) // CHUNK, chunk, 0)

    for x in range(nx):
        column[pl.ds(x, 1), :] = jnp.sum(acc[HALO + x], axis=0, keepdims=True) * sens_scale


def main_call(flags, scatter, deriv, pk, fl, fr, hl, hr):
    cz, nx = pk.shape[0], pk.shape[1]
    ports = scatter.shape[1]
    ne = nx + 2 * HALO
    nb = ne // GROUP + 1
    total = ne + nb
    return pl.pallas_call(
        main_kernel,
        in_specs=[SMEM, VMEM, VMEM, ANY, VMEM, VMEM, ANY, ANY],
        out_specs=[VMEM, VMEM],
        out_shape=[
            jax.ShapeDtypeStruct((ports, cz, nx, LANES), F32),
            jax.ShapeDtypeStruct((nx, LANES), F32),
        ],
        scratch_shapes=[
            pltpu.VMEM((cz, total, ROWS, LANES), F32),
            pltpu.VMEM((cz, total, ROWS, LANES), F32),
            pltpu.VMEM((cz, total, ROWS, LANES), F32),
            pltpu.VMEM((cz, total, ROWS, LANES), F32),
            pltpu.VMEM((cz, total, SUB, LANES), F32),
            pltpu.VMEM((cz, total, 80, LANES), BF16),
            pltpu.VMEM((2, cz, ne, ROWS, LANES), F32),
            pltpu.VMEM((2, cz, ne, ROWS, LANES), F32),
            pltpu.VMEM((cz, nb, SUB, LANES), F32),
            pltpu.VMEM((cz, nb, SUB, LANES), F32),
            pltpu.VMEM((cz, nb, SUB, LANES), F32),
            pltpu.VMEM((cz, nb, SUB, LANES), F32),
            pltpu.VMEM((ne, SUB, LANES), F32),
            pltpu.VMEM((8 * ROWS, KDIM), F32),
            pltpu.VMEM((2, DEEP, MSG, LANES), F32),
            pltpu.SemaphoreType.DMA((3 + 8 * DEEP,)),
        ],
        compiler_params=pltpu.CompilerParams(vmem_limit_bytes=63 * MIB),
        name="adjoint_steps",
    )(flags, scatter, deriv, pk, fl, fr, hl, hr)


def route_kernel(ids, ranks, id_slots):
    nx = ids.shape[0]
    ndev, cap = id_slots.shape
    owned = nx * LANES
    who = iota((ndev, LANES), 0)
    place = iota((cap, LANES), 0)
    before = (iota((LANES, LANES), 0) < iota((LANES, LANES), 1)).astype(BF16)
    offset = jnp.zeros((ndev, 1), F32)
    id_slots[...] = jnp.zeros_like(id_slots)
    for x in range(nx):
        wanted = ids[pl.ds(x, 1), :]
        hot = (wanted // owned == who).astype(F32)
        counts = jnp.dot(hot.astype(BF16), before, preferred_element_type=F32) + offset
        rank = jnp.sum(hot * counts, axis=0, keepdims=True).astype(jnp.int32)
        ranked = (rank == place).astype(F32).astype(BF16)
        offset = offset + jnp.sum(hot, axis=1, keepdims=True)
        local = wanted % owned
        ranks[pl.ds(x, 1), :] = rank
        high = (hot * (local // 64).astype(F32)).astype(BF16)
        low = (hot * (local % 64).astype(F32)).astype(BF16)
        both = lax.dot_general(
            jnp.concatenate([high, low], axis=0), ranked, (((1,), (1,)), ((), ())), preferred_element_type=F32
        )
        id_slots[...] += 64.0 * both[:ndev] + both[ndev:]


def route(ids, ndev, cap):
    return pl.pallas_call(
        route_kernel,
        in_specs=[VMEM],
        out_specs=[VMEM] * 2,
        out_shape=[
            jax.ShapeDtypeStruct(ids.shape, jnp.int32),
            jax.ShapeDtypeStruct((ndev, cap), F32),
        ],
        compiler_params=pltpu.CompilerParams(vmem_limit_bytes=24 * MIB),
        name="route",
    )(ids)


def send_kernel(column, ids, ranks, id_slots, message):
    nx = column.shape[0]
    ndev, cap = id_slots.shape
    owned = nx * LANES
    who = iota((ndev, LANES), 0)
    place = iota((cap, LANES), 0)
    total = jnp.zeros((2 * ndev, cap), F32)
    for x in range(nx):
        value = jnp.broadcast_to(column[pl.ds(x, 1), :], (ndev, LANES))
        high = value.astype(BF16).astype(F32)
        mine = ids[pl.ds(x, 1), :] // owned == who
        left = jnp.concatenate([jnp.where(mine, high, 0.0), jnp.where(mine, value - high, 0.0)], axis=0)
        ranked = (ranks[pl.ds(x, 1), :] == place).astype(F32).astype(BF16)
        total = total + lax.dot_general(
            left.astype(BF16), ranked, (((1,), (1,)), ((), ())), preferred_element_type=F32
        )
    message[:, pl.ds(0, cap)] = total[:ndev] + total[ndev:]
    message[:, pl.ds(cap, cap)] = id_slots[...]


def send(column, ids, ranks, id_slots):
    ndev, cap = id_slots.shape
    return pl.pallas_call(
        send_kernel,
        in_specs=[VMEM] * 4,
        out_specs=VMEM,
        out_shape=jax.ShapeDtypeStruct((ndev, 2 * cap), F32),
        compiler_params=pltpu.CompilerParams(vmem_limit_bytes=24 * MIB),
        name="send",
    )(column, ids, ranks, id_slots)


def gather_kernel(message, out):
    ndev, cap = message.shape[0], message.shape[1] // 2
    nrow = out.shape[0]
    rows = iota((nrow, cap), 0)
    lanes = iota((LANES, cap), 0)
    total = jnp.zeros((2 * nrow, LANES), F32)
    for s in range(ndev):
        value = jnp.broadcast_to(message[pl.ds(s, 1), pl.ds(0, cap)], (nrow, cap))
        local = message[pl.ds(s, 1), pl.ds(cap, cap)].astype(jnp.int32)
        high = value.astype(BF16).astype(F32)
        mine = local // LANES == rows
        left = jnp.concatenate([jnp.where(mine, high, 0.0), jnp.where(mine, value - high, 0.0)], axis=0)
        right = (local % LANES == lanes).astype(F32).astype(BF16)
        total = total + lax.dot_general(
            left.astype(BF16), right, (((1,), (1,)), ((), ())), preferred_element_type=F32
        )
    out[...] = total[:nrow] + total[nrow:]


def gather(message, owned):
    return pl.pallas_call(
        gather_kernel,
        in_specs=[VMEM],
        out_specs=VMEM,
        out_shape=jax.ShapeDtypeStruct((owned // LANES, LANES), F32),
        compiler_params=pltpu.CompilerParams(vmem_limit_bytes=24 * MIB),
        name="gather",
    )(message)


def moved(block, axis, distance, wrap):
    count = lax.axis_size(axis)
    pairs = [(i, (i + distance) % count) for i in range(count) if wrap or 0 <= i + distance < count]
    return lax.ppermute(block, axis, pairs)


def shards(incident, cotangent, scatter_table, deriv_table, material_code, boundary_code, param_ids):
    position = lax.axis_index("gy")
    extent = lax.axis_size("gy")
    ndev = lax.axis_size("gx") * extent
    owned = param_ids.shape[0] * param_ids.shape[1]
    cap = 2 * owned // ndev
    pk, up, down, xl, xr = pack(
        incident, cotangent, jnp.swapaxes(material_code, 1, 2), jnp.swapaxes(boundary_code, 1, 2)
    )
    fl = moved(up, "gy", 1, False)
    fr = moved(down, "gy", -1, False)
    ranks, id_slots = route(param_ids, ndev, cap)
    xl, xr = corners(fl, fr, xl, xr)
    hr = moved(xl, "gx", -1, True)
    hl = moved(xr, "gx", 1, True)
    flags = jnp.stack([position == 0, position == extent - 1]).astype(jnp.int32)
    adjoint, column = main_call(flags, scatter_table, deriv_table, pk, fl, fr, hl, hr)
    message = send(column, param_ids, ranks, id_slots)
    received = lax.all_to_all(message, ("gx", "gy"), 0, 0, tiled=True)
    sensitivity = gather(received, owned).reshape(-1)
    return adjoint, sensitivity


def solution(mesh):
    in_specs = (
        P(None, None, "gx", "gy"),
        P(None, None, "gx", "gy"),
        P(),
        P(),
        P(None, "gx", "gy"),
        P(None, "gx", "gy"),
        P("gx", "gy"),
    )
    out_specs = (P(None, None, "gx", "gy"), P(("gx", "gy")))
    return jax.shard_map(shards, mesh=mesh, in_specs=in_specs, out_specs=out_specs, check_vma=False)
```

```python
import functools

import jax
import jax.numpy as jnp
from jax import lax
from jax.experimental import pallas as pl
from jax.experimental.pallas import tpu as pltpu
from jax.sharding import PartitionSpec as P

BW = 8
ITERS = 4
CHUNK = 16
PACK_VMEM = 60
HALO = 4
SUB = 8
LANES = 128
GROUP = LANES // (2 * HALO)
MSG = 40
DEEP = 3
ROWS = 24
KDIM = 144
F32 = jnp.float32
BF16 = jnp.bfloat16
sens_scale = 1.0 / 32.0
MIB = 2**20
VMEM = pl.BlockSpec(memory_space=pltpu.VMEM)
SMEM = pl.BlockSpec(memory_space=pltpu.SMEM)
ANY = pl.BlockSpec(memory_space=pl.ANY)


def iota(shape, dim):
    return lax.broadcasted_iota(jnp.int32, shape, dim)


def roll(value, amount, axis):
    return pltpu.roll(value, amount, axis)


def shifted(block):
    row = iota((SUB, LANES), 0)
    up = roll(block, LANES - 1, 1)
    down = roll(block, 1, 1)
    return jnp.where(row < 4, block, jnp.where(row < 6, up, down))


def swap_pairs(block):
    row = iota((SUB, LANES), 0)
    return jnp.where(row % 4 < 2, roll(block, SUB - 2, 0), roll(block, 2, 0))


def swap_first(block):
    row = iota((SUB, LANES), 0)
    return jnp.where(row < 4, swap_pairs(block), block)


def near_lanes(first):
    lane = iota((SUB, LANES), 1)
    x = jnp.clip(first + lane // (2 * HALO), 0, LANES // HALO - 1)
    c = lane % HALO
    return HALO * x + c, HALO * ((x + 1) % (LANES // HALO)) + c


def pick(below, above, lanes):
    lane = iota((SUB, LANES), 1)
    below = jnp.take_along_axis(below, lanes[0], axis=1)
    above = jnp.take_along_axis(above, lanes[1], axis=1)
    return jnp.where(lane % (2 * HALO) < HALO, below, above)


def pack_kernel(inc, cot, mat, ends, pk, up, down, xl, xr):
    z = pl.program_id(0)
    cz = pl.num_programs(0)
    nx = inc.shape[2]
    lane = iota((SUB, LANES), 1)
    row = iota((SUB, LANES), 0)
    width = mat.shape[1]
    spread = (iota((width, LANES), 1) // BW == iota((width, LANES), 0)).astype(F32).astype(BF16)

    def expand(codes):
        dims = (((0,), (0,)), ((), ()))
        return lax.dot_general(codes.astype(F32).astype(BF16), spread, dims, preferred_element_type=F32)

    def coefficient(codes):
        return jnp.where(codes == 0, -1.0, jnp.where(codes == 1, 1.0, 0.0))

    code = expand(mat[0])
    lower = expand(coefficient(ends[0]))
    upper = expand(coefficient(ends[1]))
    end = jnp.where(z == 0, lower, jnp.where(z == cz - 1, upper, 0.0))
    flat_inc = inc.reshape(inc.shape[0] * nx, LANES)
    flat_cot = cot.reshape(cot.shape[0] * nx, LANES)
    to_up = [jnp.zeros((SUB, LANES), F32) for _ in range(5)]
    to_down = [jnp.zeros((SUB, LANES), F32) for _ in range(5)]
    firsts = {}
    for x in range(nx):
        f0 = flat_inc[pl.ds(x, 8, stride=nx), :]
        f1 = flat_inc[pl.ds(8 * nx + x, 8, stride=nx), :]
        a0 = swap_pairs(flat_cot[pl.ds(x, 8, stride=nx), :])
        a1 = swap_first(flat_cot[pl.ds(8 * nx + x, 8, stride=nx), :])
        last = [
            flat_inc[pl.ds(16 * nx + x, 1), :],
            flat_inc[pl.ds(17 * nx + x, 1), :],
            flat_cot[pl.ds(16 * nx + x, 1), :],
            flat_cot[pl.ds(17 * nx + x, 1), :],
            code[x : x + 1],
            end[x : x + 1],
        ]
        tail = jnp.zeros((SUB, LANES), F32)
        for i, value in enumerate(last):
            tail = jnp.where(row == i, jnp.broadcast_to(value, (SUB, LANES)), tail)
        group = lane // HALO
        for i, value in enumerate((f0, f1, a0, a1, tail)):
            turned = roll(value, (HALO * x + HALO) % LANES, 1) if x + 1 < nx else value
            to_up[i] = jnp.where(group == x, turned, to_up[i])
            to_down[i] = jnp.where(group == (x + 1) % nx, turned, to_down[i])
        firsts[x] = a0
        for i, value in enumerate((f0, f1, shifted(a0), a1, tail)):
            pk[0, x, pl.ds(8 * i, 8), :] = value
            if x < DEEP:
                xl[0, pl.ds(MSG * x + 8 * i, 8), :] = value
            if x >= nx - DEEP:
                xr[0, pl.ds(MSG * (x - nx + DEEP) + 8 * i, 8), :] = value
    xl[0, pl.ds(DEEP * MSG - 2, 2), :] = firsts[DEEP][0:2]
    xr[0, pl.ds(MSG - 2, 2), :] = firsts[nx - DEEP - 1][2:4]
    for i in range(5):
        up[0, pl.ds(8 * i, 8), :] = to_up[i]
        down[0, pl.ds(8 * i, 8), :] = to_down[i]


def pack(incident, cotangent, material, ends):
    ports, cz, nx, ny = incident.shape
    field = pl.BlockSpec((ports, 1, nx, ny), lambda z: (0, z, 0, 0))
    codes = pl.BlockSpec((1,) + material.shape[1:], lambda z: (z, 0, 0))
    both = pl.BlockSpec(ends.shape, lambda z: (0, 0, 0))
    edge = pl.BlockSpec((1, MSG, LANES), lambda z: (z, 0, 0))
    deep = pl.BlockSpec((1, DEEP * MSG, LANES), lambda z: (z, 0, 0))
    return pl.pallas_call(
        pack_kernel,
        grid=(cz,),
        in_specs=[field, field, codes, both],
        out_specs=[pl.BlockSpec((1, nx, MSG, LANES), lambda z: (z, 0, 0, 0)), edge, edge, deep, deep],
        out_shape=[
            jax.ShapeDtypeStruct((cz, nx, MSG, LANES), F32),
            jax.ShapeDtypeStruct((cz, MSG, LANES), F32),
            jax.ShapeDtypeStruct((cz, MSG, LANES), F32),
            jax.ShapeDtypeStruct((cz + 1, DEEP * MSG, LANES), F32),
            jax.ShapeDtypeStruct((cz + 1, DEEP * MSG, LANES), F32),
        ],
        compiler_params=pltpu.CompilerParams(vmem_limit_bytes=PACK_VMEM * MIB),
        name="pack",
    )(incident, cotangent, material, ends)


def corner_kernel(below, above, xl_in, xr_in, xl, xr, left, right, sems):
    cz = below.shape[0]
    nx = LANES // HALO
    lane = iota((SUB, LANES), 1)
    x = (lane % 32) // (2 * HALO)
    c = lane % HALO

    def lanes(first):
        return HALO * (first + x) + c, HALO * ((first + x + 1) % nx) + c

    low, high = lanes(0), lanes(nx - HALO)
    for out, place in ((left, low), (right, high)):
        for q in range(DEEP):
            for i in range(5):
                part = pl.ds(8 * i, 8)
                value = jnp.zeros((SUB, LANES), F32)
                for h in range(4):
                    z = 4 * q + h
                    if z < cz:
                        value = jnp.where(lane // 32 == h, pick(below[z, part, :], above[z, part, :], place), value)
                out[pl.ds(MSG * q + 8 * i, 8), :] = value
    copies = [
        pltpu.make_async_copy(left, xl.at[cz], sems.at[0]),
        pltpu.make_async_copy(right, xr.at[cz], sems.at[1]),
    ]
    for copy in copies:
        copy.start()
    for copy in copies:
        copy.wait()


def corners(below, above, xl, xr):
    shape = jax.ShapeDtypeStruct(xl.shape, F32)
    return pl.pallas_call(
        corner_kernel,
        in_specs=[VMEM, VMEM, ANY, ANY],
        out_specs=[ANY, ANY],
        out_shape=[shape, shape],
        input_output_aliases={2: 0, 3: 1},
        scratch_shapes=[
            pltpu.VMEM((DEEP * MSG, LANES), F32),
            pltpu.VMEM((DEEP * MSG, LANES), F32),
            pltpu.SemaphoreType.DMA((2,)),
        ],
        compiler_params=pltpu.CompilerParams(vmem_limit_bytes=16 * MIB),
        name="corners",
    )(below, above, xl, xr)


def build_tables(scatter, deriv, tables):
    nmat, ports, _ = scatter.shape
    r = iota((ROWS, ports), 0)
    c = iota((ROWS, ports), 1)
    tail = (r >= 16) & (c == 16 + r % 2)
    natural = (((r < 16) & (r == c)) | tail).astype(F32).astype(BF16)
    swapped_port = jnp.where(r < 12, r + jnp.where(r % 4 < 2, 2, -2), r)
    permuted = (((r < 16) & (swapped_port == c)) | tail).astype(F32).astype(BF16)
    plain = (r == c).astype(F32).astype(BF16)
    q = iota((ports, KDIM), 0)
    k = iota((ports, KDIM), 1)

    def place(m):
        main = (k < 128) & ((k // 16) % 4 == m) & (q == k % 16)
        end = (k >= 128) & ((k % 8) // 2 == m) & (q == 16 + k % 2)
        return (main | end).astype(F32).astype(BF16)

    places = [place(m) for m in range(nmat)]

    def split(value):
        high = value.astype(BF16)
        return high, (value - high.astype(F32)).astype(BF16)

    def form(table, rows, transpose):
        parts = []
        for part in range(2):
            total = jnp.zeros((ROWS, KDIM), F32)
            for m in range(nmat):
                piece = split(table[m])[part]
                axes = (((1,), (1 if transpose else 0,)), ((), ()))
                picked = lax.dot_general(rows, piece, axes, preferred_element_type=F32).astype(BF16)
                total = total + jnp.dot(picked, places[m], preferred_element_type=F32)
            parts.append(total.astype(BF16))
        return parts

    forms = (
        form(scatter, permuted, False)
        + form(deriv, plain, False)
        + form(scatter, permuted, True)
        + form(scatter, natural, True)
    )
    for i, value in enumerate(forms):
        tables[pl.ds(ROWS * i, ROWS), :] = value.astype(F32)


def repeated(value):
    row = iota((SUB, LANES), 0)
    value = jnp.where(row < 2, value, 0.0)
    value = value + roll(value, 2, 0)
    return value + roll(value, 4, 0)


def masks_of(code):
    code = jnp.broadcast_to(code, (16, LANES))
    own = ((iota((16, LANES), 0) % 8) // 2).astype(F32)
    return [jnp.where(code == m, 1.0, 0.0).astype(BF16) for m in (0, 1, 2, 3, own)]


def collect(x, z, e, block):
    lane = iota((SUB, LANES), 1)
    g = e % GROUP
    moved_block = roll(block, 8 * g + HALO, 1)
    x[z, e // GROUP] = jnp.where(lane // 8 == g, moved_block, x[z, e // GROUP])


def in_pairs(cz, before, after):
    pending = None
    for z in range(0, cz, 2):
        made = before(z)
        if pending is not None:
            after(*pending)
        pending = (z, made)
    after(*pending)


def operand(values, mask):
    v0, v1, v2 = values
    main = jnp.concatenate([v0, v1], axis=0)
    high = main.astype(BF16)
    low = (main - high.astype(F32)).astype(BF16)
    high2 = v2.astype(BF16).astype(F32)
    end = jnp.concatenate([high2, v2 - high2], axis=0).astype(BF16)
    pieces = [high * mask[m] for m in range(4)] + [low * mask[m] for m in range(4)]
    return jnp.concatenate(pieces + [end * mask[4]], axis=0)


def apply(table, values, mask):
    rhs = jnp.concatenate([operand(values[h], mask[h]) for h in range(2)], axis=1)
    y = jnp.dot(table, rhs, preferred_element_type=F32)
    outs = []
    for h in range(2):
        part = y[:, h * LANES : (h + 1) * LANES]
        outs.append([
            [part[at + 8 * i : at + 8 * i + 8] + part[at + ROWS + 8 * i : at + ROWS + 8 * i + 8] for i in range(3)]
            for at in range(0, table.shape[0], 2 * ROWS)
        ])
    return outs


def prep_kernel(scatter, deriv, pk, tables, masks, first, change, tails, xf, xa):
    c = pl.program_id(0)
    cz, rows = pk.shape[0], pk.shape[1]

    @pl.when(c == 0)
    def _():
        build_tables(scatter, deriv, tables)
        xf[...] = jnp.zeros_like(xf)
        xa[...] = jnp.zeros_like(xa)

    f_table = tables[pl.ds(0, 4 * ROWS), :].astype(BF16)
    for x in range(rows):
        e = c * rows + x + HALO

        def before(z, x=x, e=e):
            mask, values = [], []
            for h in range(2):
                t = pk[z + h, x, pl.ds(32, 8), :]
                tails[z + h, x] = repeated(roll(t, 6, 0))
                mask.append(masks_of(pk[z + h, x, pl.ds(36, 1), :]))
                for m, value in enumerate(mask[h]):
                    masks[z + h, x, pl.ds(16 * m, 16), :] = value
                values.append([pk[z + h, x, pl.ds(0, 8), :], pk[z + h, x, pl.ds(8, 8), :], repeated(t)])
                collect(xa, z + h, e, pk[z + h, x, pl.ds(16, 8), :])
            return apply(f_table, values, mask)

        def after(z, made, x=x, e=e):
            for h in range(2):
                part, other = made[h]
                outer = shifted(part[0])
                collect(xf, z + h, e, outer)
                for i, value in enumerate((outer, part[1], part[2])):
                    first[z + h, x, pl.ds(8 * i, 8), :] = value
                for i, value in enumerate(other):
                    change[z + h, x, pl.ds(8 * i, 8), :] = value

        in_pairs(cz, before, after)


def prep(scatter, deriv, pk):
    cz, nx = pk.shape[0], pk.shape[1]
    rows = 8
    nb = (nx + 2 * HALO) // GROUP + 1

    def by_rows(depth):
        return pl.BlockSpec((cz, rows, depth, LANES), lambda c: (0, c, 0, 0))

    table = pl.BlockSpec(scatter.shape, lambda c: (0, 0, 0))
    edge = pl.BlockSpec((cz, nb, SUB, LANES), lambda c: (0, 0, 0, 0))
    edges = jax.ShapeDtypeStruct((cz, nb, SUB, LANES), F32)
    return pl.pallas_call(
        prep_kernel,
        grid=(nx // rows,),
        in_specs=[table, table, by_rows(MSG)],
        out_specs=[
            pl.BlockSpec((8 * ROWS, KDIM), lambda c: (0, 0)),
            by_rows(80), by_rows(ROWS), by_rows(ROWS), by_rows(SUB), edge, edge,
        ],
        out_shape=[
            jax.ShapeDtypeStruct((8 * ROWS, KDIM), F32),
            jax.ShapeDtypeStruct((cz, nx, 80, LANES), BF16),
            jax.ShapeDtypeStruct((cz, nx, ROWS, LANES), F32),
            jax.ShapeDtypeStruct((cz, nx, ROWS, LANES), F32),
            jax.ShapeDtypeStruct((cz, nx, SUB, LANES), F32),
            edges,
            edges,
        ],
        compiler_params=pltpu.CompilerParams(vmem_limit_bytes=PACK_VMEM * MIB),
        cost_estimate=pl.CostEstimate(flops=2 * 10**9, bytes_accessed=24 * 10**6, transcendentals=0),
        name="prep",
    )(scatter, deriv, pk)


def main_kernel(
    flags, tables, xf_in, xa_in, pk, own_masks, first_in, change_in, tails_in, fl, fr, hl, hr,
    adjoint, column,
    rf0, rf1, ra0, ra1, rtail, masks, saved_d, saved_r, xf, xa, tf, ta, acc, cbuf, sems,
):
    cz, nx = pk.shape[0], pk.shape[1]
    ne = nx + 2 * HALO
    nb = rf0.shape[1] - ne
    rf, ra = (rf0, rf1), (ra0, ra1)
    row = iota((SUB, LANES), 0)
    lane = iota((SUB, LANES), 1)
    is_first = flags[0] == 1
    is_last = flags[1] == 1

    copies = []

    def bring(source, target):
        copies.append(pltpu.make_async_copy(source, target, sems.at[len(copies)]))

    own = pl.ds(HALO, nx)
    bring(pk.at[:, :, pl.ds(16, 16)], ra0.at[:, own, pl.ds(0, 16)])
    bring(tails_in, ra0.at[:, own, pl.ds(16, 8)])
    bring(own_masks, masks.at[:, own])
    bring(pk.at[:, :, pl.ds(32, 8)], rtail.at[:, pl.ds(HALO, nx)])
    for source, first in ((hl, HALO - DEEP), (hr, HALO + nx)):
        for i in range(DEEP):
            for buffer, at in ((rf0, 0), (ra0, 16)):
                bring(source.at[pl.ds(0, cz), pl.ds(MSG * i + at, 16)], buffer.at[:, first + i, pl.ds(0, 16)])
            bring(source.at[pl.ds(0, cz), pl.ds(MSG * i + 32, 8)], rtail.at[:, first + i])
    for q in range(DEEP):
        for i, source in enumerate((hl, hr)):
            bring(source.at[cz, pl.ds(MSG * q, MSG)], cbuf.at[i, q])
    halo_copies = len(copies)
    bring(first_in, rf1.at[:, own])
    bring(change_in, saved_d.at[0, :, own])
    order = copies[4:halo_copies] + copies[:4] + copies[halo_copies:]
    for copy in order:
        copy.start()
    xf[...] = xf_in[...]
    xa[...] = xa_in[...]
    for copy in copies[4:halo_copies]:
        copy.wait()

    places = [near_lanes(GROUP * b - HALO) for b in range(nb)]

    def halo_blocks(z, _):
        turn = LANES - 32 * (z % 4)
        for i in range(5):
            part = pl.ds(8 * i, 8)
            for b in range(nb):
                value = pick(fl[z, part, :], fr[z, part, :], places[b])
                if b == 0:
                    outer = roll(cbuf[0, z // 4, part, :], turn % LANES, 1)
                    value = jnp.where(lane < 8 * HALO, outer, value)
                if b == nb - 1:
                    outer = roll(cbuf[1, z // 4, part, :], (turn + 32) % LANES, 1)
                    value = jnp.where(lane < 8 * HALO, value, outer)
                if i == 0 or i == 1:
                    rf0[z, ne + b, part, :] = value
                elif i == 2:
                    ra0[z, ne + b, pl.ds(0, 8), :] = shifted(value)
                elif i == 3:
                    ra0[z, ne + b, pl.ds(8, 8), :] = value
                else:
                    rtail[z, ne + b] = value
        ra0[z, 0, pl.ds(0, 8), :] = roll(rtail[z, HALO - DEEP], 4, 0)
        ra0[z, ne - 1, pl.ds(0, 8), :] = roll(rtail[z, ne - 1 - (HALO - DEEP)], 2, 0)
        return 0

    lax.fori_loop(0, cz, halo_blocks, 0, unroll=2)

    def start_row(r, _):
        for z in range(cz):
            t = rtail[z, r]
            rf0[z, r, pl.ds(16, 8), :] = repeated(t)
            ra0[z, r, pl.ds(16, 8), :] = repeated(roll(t, 6, 0))
            for m, value in enumerate(masks_of(rtail[z, r, pl.ds(4, 1), :])):
                masks[z, r, pl.ds(16 * m, 16), :] = value
        return 0

    outer_rows = list(range(HALO)) + list(range(HALO + nx, ne))
    for r in outer_rows + [ne + b for b in range(nb)]:
        start_row(r, 0)

    def mask_of(z, r):
        return [masks[z, r, pl.ds(16 * m, 16), :] for m in range(5)]

    def load(ref, z, r, i):
        return ref[z, r, pl.ds(8 * i, 8), :]

    def read(ref, z, r):
        return [load(ref, z, r, i) for i in range(3)]

    def along_z(ref, z, r):
        own = load(ref, z, r, 1)
        if z + 1 < cz:
            above = load(ref, z + 1, r, 1)
        else:
            above = jnp.broadcast_to(rtail[z, r, pl.ds(5, 1), :], (SUB, LANES)) * roll(own, 6, 0)
        if z > 0:
            below = load(ref, z - 1, r, 1)
        else:
            below = jnp.broadcast_to(rtail[z, r, pl.ds(5, 1), :], (SUB, LANES)) * roll(own, 2, 0)
        return jnp.where(row < 2, above, jnp.where(row < 4, below, own))

    at_ends = ((row // 2 == 2) & (lane == LANES - 1)) | ((row // 2 == 3) & (lane == 0))
    at_edges = ((row // 2 == 2) & (lane % 8 == HALO - 1)) | ((row // 2 == 3) & (lane % 8 == HALO))

    def connect_row(ref, tm, z, e):
        amount = LANES - (8 * (e % GROUP) + HALO)
        outer = roll(tm[z, e // GROUP], amount, 1)
        own = jnp.where(at_ends, outer, load(ref, z, e, 0))
        first = jnp.where(row < 2, load(ref, z, e + 1, 0), jnp.where(row < 4, load(ref, z, e - 1, 0), own))
        return [first, along_z(ref, z, e), load(ref, z, e, 2)]

    def connect_edge(ref, x, tm, z, b):
        own = load(ref, z, ne + b, 0)
        nxt = load(ref, z, ne + (b + 1) % nb, 0)
        prv = load(ref, z, ne + (b + nb - 1) % nb, 0)
        after = roll(jnp.where(lane >= 8, own, nxt), LANES - 8, 1)
        before = roll(jnp.where(lane < LANES - 8, own, prv), 8, 1)
        inner = x[z, b]
        top = roll(roll(inner, LANES - 1, 1), 6, 0)
        bottom = roll(roll(inner, 1, 1), 2, 0)
        tm[z, b] = jnp.where(is_last & (row < 6), -top, jnp.where(is_first & (row >= 6), -bottom, own))
        own = jnp.where(at_edges, inner, own)
        first = jnp.where(row < 2, after, jnp.where(row < 4, before, own))
        return [first, along_z(ref, z, ne + b), load(ref, z, ne + b, 2)]

    def write(ref, z, r, part):
        first = shifted(part[0])
        ref[z, r, pl.ds(0, 8), :] = first
        ref[z, r, pl.ds(8, 8), :] = part[1]
        ref[z, r, pl.ds(16, 8), :] = part[2]
        return first

    for e in outer_rows:
        for z in range(cz):
            collect(xa, z, e, ra0[z, e, pl.ds(0, 8), :])
    for copy in copies[:4]:
        copy.wait()
    flat = adjoint.reshape(adjoint.shape[0] * cz * nx, LANES)

    for step in range(ITERS):
        fa, ta_, fb, tb = rf[step % 2], ra[step % 2], rf[(step + 1) % 2], ra[(step + 1) % 2]
        last = step == ITERS - 1
        a_table = tables[pl.ds((6 if last else 4) * ROWS, 2 * ROWS), :].astype(BF16)
        if last:
            f_table = tables[pl.ds(2 * ROWS, 2 * ROWS), :].astype(BF16)
        else:
            f_table = tables[pl.ds(0, 4 * ROWS), :].astype(BF16)
        s_table = tables[pl.ds(0, 2 * ROWS), :].astype(BF16)

        for b in range(nb):
            def before(z, b=b):
                av = [connect_edge(ta_, xa, ta, z + h, b) for h in range(2)]
                if step > 0:
                    fv = [connect_edge(fa, xf, tf, z + h, b) for h in range(2)]
                else:
                    fv = [read(fa, z + h, ne + b) for h in range(2)]
                if last:
                    return None
                mask = [mask_of(z + h, ne + b) for h in range(2)]
                return apply(a_table, av, mask), apply(s_table, fv, mask)

            def after(z, made, b=b):
                if last:
                    return
                for h in range(2):
                    write(tb, z + h, ne + b, made[0][h][0])
                    write(fb, z + h, ne + b, made[1][h][0])

            in_pairs(cz, before, after)

        def rows(e, outer=False):
            total = []

            def before(z):
                mask = [mask_of(z + h, e) for h in range(2)]
                av = [connect_row(ta_, ta, z + h, e) for h in range(2)]
                a_out = apply(a_table, av, mask)
                if step < 2:
                    for h in range(2):
                        for i in range(3):
                            saved_r[step, z + h, e, pl.ds(8 * i, 8), :] = av[h][i]
                else:
                    for h in range(2):
                        for i in range(3):
                            total.append(av[h][i] * load(saved_d.at[ITERS - 1 - step], z + h, e, i))
                if step > 0:
                    fv = [connect_row(fa, tf, z + h, e) for h in range(2)]
                    return a_out, apply(f_table, fv, mask)
                if outer:
                    fv = [read(fa, z + h, e) for h in range(2)]
                    return a_out, apply(s_table, fv, mask)
                return a_out, None

            def after(z, made):
                a_out, f_out = made
                for h in range(2):
                    part = a_out[h][0]
                    if last:
                        at = (z + h) * nx + e - HALO
                        flat[pl.ds(at, 8, stride=cz * nx), :] = part[0]
                        flat[pl.ds(8 * cz * nx + at, 8, stride=cz * nx), :] = part[1]
                        flat[pl.ds(16 * cz * nx + at, 1), :] = part[2][0:1]
                        flat[pl.ds(17 * cz * nx + at, 1), :] = part[2][1:2]
                        change = f_out[h][0]
                    else:
                        collect(xa, z + h, e, write(tb, z + h, e, part))
                        if f_out is None:
                            continue
                        collect(xf, z + h, e, write(fb, z + h, e, f_out[h][0]))
                        if step == 0:
                            continue
                        change = f_out[h][1]
                    for i in range(3):
                        if step < 2:
                            saved_d[step, z + h, e, pl.ds(8 * i, 8), :] = change[i]
                        else:
                            total.append(change[i] * load(saved_r.at[ITERS - 1 - step], z + h, e, i))
                if total:
                    value = functools.reduce(lambda p, q: p + q, total)
                    del total[:]
                    total.append(value)

            in_pairs(cz, before, after)
            if step == 2:
                acc[e] = total[0]
            elif step > 2:
                acc[e] = acc[e] + total[0]
            return 0

        begin, end = 1 + step, ne - 1 - step
        if step == 0:
            begin, spare = HALO, [r for r in outer_rows if begin <= r < end]
        else:
            spare = list(range(begin, begin + (end - begin) % CHUNK))
            begin += len(spare)
        for e in spare:
            rows(e, step == 0)

        def chunk(c, _, begin=begin):
            for i in range(CHUNK):
                rows(begin + c * CHUNK + i)
            return 0

        lax.fori_loop(0, nx // CHUNK, chunk, 0)
        if step == 0:
            copies[halo_copies].wait()
        if step == 2:
            copies[halo_copies + 1].wait()

    for x in range(nx):
        column[pl.ds(x, 1), :] = jnp.sum(acc[HALO + x], axis=0, keepdims=True) * sens_scale


def main_call(flags, ports, tables, xf, xa, pk, masks, first, change, tails, fl, fr, hl, hr):
    cz, nx = pk.shape[0], pk.shape[1]
    ne = nx + 2 * HALO
    nb = ne // GROUP + 1
    total = ne + nb
    return pl.pallas_call(
        main_kernel,
        in_specs=[SMEM, VMEM, VMEM, VMEM, ANY, ANY, ANY, ANY, ANY, VMEM, VMEM, ANY, ANY],
        out_specs=[VMEM, VMEM],
        out_shape=[
            jax.ShapeDtypeStruct((ports, cz, nx, LANES), F32),
            jax.ShapeDtypeStruct((nx, LANES), F32),
        ],
        scratch_shapes=[
            pltpu.VMEM((cz, total, ROWS, LANES), F32),
            pltpu.VMEM((cz, total, ROWS, LANES), F32),
            pltpu.VMEM((cz, total, ROWS, LANES), F32),
            pltpu.VMEM((cz, total, ROWS, LANES), F32),
            pltpu.VMEM((cz, total, SUB, LANES), F32),
            pltpu.VMEM((cz, total, 80, LANES), BF16),
            pltpu.VMEM((2, cz, ne, ROWS, LANES), F32),
            pltpu.VMEM((2, cz, ne, ROWS, LANES), F32),
            pltpu.VMEM((cz, nb, SUB, LANES), F32),
            pltpu.VMEM((cz, nb, SUB, LANES), F32),
            pltpu.VMEM((cz, nb, SUB, LANES), F32),
            pltpu.VMEM((cz, nb, SUB, LANES), F32),
            pltpu.VMEM((ne, SUB, LANES), F32),
            pltpu.VMEM((2, DEEP, MSG, LANES), F32),
            pltpu.SemaphoreType.DMA((6 + 8 * DEEP,)),
        ],
        compiler_params=pltpu.CompilerParams(vmem_limit_bytes=63 * MIB),
        name="adjoint_steps",
    )(flags, tables, xf, xa, pk, masks, first, change, tails, fl, fr, hl, hr)


def route_kernel(ids, ranks, id_slots):
    nx = ids.shape[0]
    ndev, cap = id_slots.shape
    owned = nx * LANES
    who = iota((ndev, LANES), 0)
    place = iota((cap, LANES), 0)
    before = (iota((LANES, LANES), 0) < iota((LANES, LANES), 1)).astype(BF16)
    offset = jnp.zeros((ndev, 1), F32)
    id_slots[...] = jnp.zeros_like(id_slots)
    for x in range(nx):
        wanted = ids[pl.ds(x, 1), :]
        hot = (wanted // owned == who).astype(F32)
        counts = jnp.dot(hot.astype(BF16), before, preferred_element_type=F32) + offset
        rank = jnp.sum(hot * counts, axis=0, keepdims=True).astype(jnp.int32)
        ranked = (rank == place).astype(F32).astype(BF16)
        offset = offset + jnp.sum(hot, axis=1, keepdims=True)
        local = wanted % owned
        ranks[pl.ds(x, 1), :] = rank
        high = (hot * (local // 64).astype(F32)).astype(BF16)
        low = (hot * (local % 64).astype(F32)).astype(BF16)
        both = lax.dot_general(
            jnp.concatenate([high, low], axis=0), ranked, (((1,), (1,)), ((), ())), preferred_element_type=F32
        )
        id_slots[...] += 64.0 * both[:ndev] + both[ndev:]


def route(ids, ndev, cap):
    return pl.pallas_call(
        route_kernel,
        in_specs=[VMEM],
        out_specs=[VMEM] * 2,
        out_shape=[
            jax.ShapeDtypeStruct(ids.shape, jnp.int32),
            jax.ShapeDtypeStruct((ndev, cap), F32),
        ],
        compiler_params=pltpu.CompilerParams(vmem_limit_bytes=24 * MIB),
        name="route",
    )(ids)


def send_kernel(column, ids, ranks, id_slots, message):
    nx = column.shape[0]
    ndev, cap = id_slots.shape
    owned = nx * LANES
    who = iota((ndev, LANES), 0)
    place = iota((cap, LANES), 0)
    total = jnp.zeros((2 * ndev, cap), F32)
    for x in range(nx):
        value = jnp.broadcast_to(column[pl.ds(x, 1), :], (ndev, LANES))
        high = value.astype(BF16).astype(F32)
        mine = ids[pl.ds(x, 1), :] // owned == who
        left = jnp.concatenate([jnp.where(mine, high, 0.0), jnp.where(mine, value - high, 0.0)], axis=0)
        ranked = (ranks[pl.ds(x, 1), :] == place).astype(F32).astype(BF16)
        total = total + lax.dot_general(
            left.astype(BF16), ranked, (((1,), (1,)), ((), ())), preferred_element_type=F32
        )
    message[:, pl.ds(0, cap)] = total[:ndev] + total[ndev:]
    message[:, pl.ds(cap, cap)] = id_slots[...]


def send(column, ids, ranks, id_slots):
    ndev, cap = id_slots.shape
    return pl.pallas_call(
        send_kernel,
        in_specs=[VMEM] * 4,
        out_specs=VMEM,
        out_shape=jax.ShapeDtypeStruct((ndev, 2 * cap), F32),
        compiler_params=pltpu.CompilerParams(vmem_limit_bytes=24 * MIB),
        name="send",
    )(column, ids, ranks, id_slots)


def gather_kernel(message, out):
    ndev, cap = message.shape[0], message.shape[1] // 2
    nrow = out.shape[0]
    rows = iota((nrow, cap), 0)
    lanes = iota((LANES, cap), 0)
    total = jnp.zeros((2 * nrow, LANES), F32)
    for s in range(ndev):
        value = jnp.broadcast_to(message[pl.ds(s, 1), pl.ds(0, cap)], (nrow, cap))
        local = message[pl.ds(s, 1), pl.ds(cap, cap)].astype(jnp.int32)
        high = value.astype(BF16).astype(F32)
        mine = local // LANES == rows
        left = jnp.concatenate([jnp.where(mine, high, 0.0), jnp.where(mine, value - high, 0.0)], axis=0)
        right = (local % LANES == lanes).astype(F32).astype(BF16)
        total = total + lax.dot_general(
            left.astype(BF16), right, (((1,), (1,)), ((), ())), preferred_element_type=F32
        )
    out[...] = total[:nrow] + total[nrow:]


def gather(message, owned):
    return pl.pallas_call(
        gather_kernel,
        in_specs=[VMEM],
        out_specs=VMEM,
        out_shape=jax.ShapeDtypeStruct((owned // LANES, LANES), F32),
        compiler_params=pltpu.CompilerParams(vmem_limit_bytes=24 * MIB),
        name="gather",
    )(message)


def moved(block, axis, distance, wrap):
    count = lax.axis_size(axis)
    pairs = [(i, (i + distance) % count) for i in range(count) if wrap or 0 <= i + distance < count]
    return lax.ppermute(block, axis, pairs)


def shards(incident, cotangent, scatter_table, deriv_table, material_code, boundary_code, param_ids):
    position = lax.axis_index("gy")
    extent = lax.axis_size("gy")
    ndev = lax.axis_size("gx") * extent
    owned = param_ids.shape[0] * param_ids.shape[1]
    cap = 2 * owned // ndev
    pk, up, down, xl, xr = pack(
        incident, cotangent, jnp.swapaxes(material_code, 1, 2), jnp.swapaxes(boundary_code, 1, 2)
    )
    fl = moved(up, "gy", 1, False)
    fr = moved(down, "gy", -1, False)
    ranks, id_slots = route(param_ids, ndev, cap)
    fl, fr, ranks, id_slots = lax.optimization_barrier((fl, fr, ranks, id_slots))
    tables, masks, first, change, tails, xf, xa = prep(scatter_table, deriv_table, pk)
    xl, xr = corners(fl, fr, xl, xr)
    hr = moved(xl, "gx", -1, True)
    hl = moved(xr, "gx", 1, True)
    flags = jnp.stack([position == 0, position == extent - 1]).astype(jnp.int32)
    adjoint, column = main_call(
        flags, scatter_table.shape[1], tables, xf, xa, pk, masks, first, change, tails, fl, fr, hl, hr
    )
    message = send(column, param_ids, ranks, id_slots)
    received = lax.all_to_all(message, ("gx", "gy"), 0, 0, tiled=True)
    sensitivity = gather(received, owned).reshape(-1)
    return adjoint, sensitivity


def solution(mesh):
    in_specs = (
        P(None, None, "gx", "gy"),
        P(None, None, "gx", "gy"),
        P(),
        P(),
        P(None, "gx", "gy"),
        P(None, "gx", "gy"),
        P("gx", "gy"),
    )
    out_specs = (P(None, None, "gx", "gy"), P(("gx", "gy")))
    return jax.shard_map(shards, mesh=mesh, in_specs=in_specs, out_specs=out_specs, check_vma=False)
```
